256 devices in a mesh: lat: 2 (over x_lo), lon: 128 (over y, x_hi, z, core).
Axes of the slice: x: 4 (x_hi: 2, x_lo: 2; x = x_hi * 2 + x_lo), y: 4, z: 8, core: 2. Of those that a mesh axis runs over, the one named last changes fastest.
Arguments:
- stream: bfloat16 [2, 48, 384, 768], P(None, 'lat', 'lon'), may hold values from -6 to 6
- land: int32 [48, 384], P('lat', 'lon'), may hold values from 0 to 16
- orography: int32 [48, 384], P('lat', 'lon'), may hold values from 0 to 7
- land_vector: float32 [768], replicated, may hold values from -6 to 6
- orography_table: float32 [8, 768], replicated, may hold values from -6 to 6
- gain_one: float32 [768], replicated, may hold values from 0.1 to 1.9
- qkv_one: bfloat16 [768, 2304], replicated, may hold values from -0.21875 to 0.21875
- proj_one: bfloat16 [768, 768], replicated, may hold values from -0.875 to 0.875
- table_one: bfloat16 [4, 12, 6336], P('lat'), may hold values from -4 to 250
- gain_two: float32 [768], replicated, may hold values from 0.1 to 1.9
- qkv_two: bfloat16 [768, 2304], replicated, may hold values from -0.21875 to 0.21875
- proj_two: bfloat16 [768, 768], replicated, may hold values from -0.875 to 0.875
- table_two: bfloat16 [4, 12, 6336], P('lat'), may hold values from -4 to 250
- cotangent: bfloat16 [2, 48, 384, 768], P(None, 'lat', 'lon'), may hold values from -6 to 6
Outputs:
- output: bfloat16 [2, 48, 384, 768], P(None, 'lat', 'lon')
- grad_stream: bfloat16 [2, 48, 384, 768], P(None, 'lat', 'lon')
The draws below stay inside these ranges and needn't reach their ends.
All inputs are finite; a program needn't handle non-finite values.
Results may differ from the reference program's by a relative error of at most 0.027.
Values may be sent and summed in bfloat16 or wider, within the bound.
No kernel may reach another device: no remote copies, remote signals or barrier semaphores. Data moves between devices by JAX's collectives and lax.ppermute only.
A program may use at most 192 MiB of HBM per device.

```python
import jax
import jax.numpy as jnp
from jax import lax

D = 768
HEADS = 12
WZ = 2
WLAT = 12
WLON = 6
LAT = 48
LON = 384
TYPES = 4
TABLE = 6336
OROG = 8
LAND = 16


def draw_table_one(key, part):
    key = jax.random.fold_in(key, 11)
    shape = (TYPES, HEADS, TABLE)
    return jnp.clip(jax.random.normal(key, shape, jnp.float32), -4.0, 4.0).astype(jnp.bfloat16)


def draw_table_two(key, part):
    key = jax.random.fold_in(key, 23)
    shape = (TYPES, HEADS, TABLE)
    return jnp.clip(jax.random.normal(key, shape, jnp.float32), -4.0, 4.0).astype(jnp.bfloat16)


def touch_ends(entries, rng, smallest, high):
    index_at = [jax.random.randint(jax.random.fold_in(rng, axis), (), 0, length) for axis, length in enumerate(entries.shape)]
    main_axis = entries.shape.index(max(entries.shape))
    beside = index_at[:main_axis] + [(index_at[main_axis] + 1) % entries.shape[main_axis]] + index_at[main_axis + 1:]
    return entries.at[tuple(index_at)].set(smallest).at[tuple(beside)].set(high)


def shard_levels(stream_key, extent, cuts, least, top_value):
    level = 1.0
    for dim, blocks in cuts:
        draws = jax.random.uniform(jax.random.fold_in(jax.random.fold_in(stream_key, 6), dim), (blocks,), jnp.float32, least / len(cuts), top_value / len(cuts))
        level = level * jnp.repeat(jnp.exp(draws), extent[dim] // blocks).reshape((-1,) + (1,) * (len(extent) - 1 - dim))
    return level


def normal_values(key, shape, deviation, limit, cuts=(), kind=jnp.bfloat16):
    values = deviation * jax.random.normal(key, shape, jnp.float32)
    if cuts:
        values = values * shard_levels(key, shape, cuts, -0.22, 0.18)
    return jnp.clip(values, -limit, limit).astype(kind)


def setup_inputs(seed: int = 0) -> dict:
    key_list = jax.random.split(jax.random.key(seed), 15)
    return {
        "stream": normal_values(key_list[0], (WZ, LAT, LON, D), 1.0, 6.0, ((1, 2), (2, 128))),
        "land": touch_ends(jax.random.randint(key_list[1], (LAT, LON), 0, LAND + 1), jax.random.fold_in(key_list[1], 1), 0, LAND).astype(jnp.int32),
        "orography": touch_ends(jax.random.randint(key_list[2], (LAT, LON), 0, OROG), jax.random.fold_in(key_list[2], 1), 0, OROG - 1).astype(jnp.int32),
        "land_vector": normal_values(key_list[3], (D,), 1.0, 6.0, (), jnp.float32),
        "orography_table": normal_values(key_list[4], (OROG, D), 1.0, 6.0, (), jnp.float32),
        "gain_one": jnp.clip(1.0 + 0.18 * jax.random.normal(key_list[5], (D,), jnp.float32), 0.1, 1.9),
        "qkv_one": normal_values(key_list[6], (D, 3 * D), D ** -0.5, 0.21875),
        "proj_one": normal_values(key_list[7], (D, D), (D // 16) ** -0.5, 0.875),
        "table_one": draw_table_one(jax.random.fold_in(key_list[14], 71), 0),
        "gain_two": jnp.clip(1.0 + 0.18 * jax.random.normal(key_list[9], (D,), jnp.float32), 0.1, 1.9),
        "qkv_two": normal_values(key_list[10], (D, 3 * D), D ** -0.5, 0.21875),
        "proj_two": normal_values(key_list[11], (D, D), (D // 16) ** -0.5, 0.875),
        "table_two": draw_table_two(jax.random.fold_in(key_list[14], 71), 0),
        "cotangent": normal_values(key_list[13], (WZ, LAT, LON, D), 1.0, 6.0, ((1, 2), (2, 128))),
    }


epsilon = 1e-05
highest = lax.Precision.HIGHEST

def layer_norm(stream, gain):
    values = stream.astype(jnp.float32)
    average = lax.optimization_barrier(jnp.mean(values, axis=-1, keepdims=True))
    centred = values - average
    inverse = lax.rsqrt(lax.optimization_barrier(jnp.mean(centred * centred, axis=-1, keepdims=True)) + epsilon)
    normed = centred * inverse
    return ((normed * gain).astype(jnp.bfloat16), normed, inverse)

def norm_back(grad_normed_in, normed, inverse, gain):
    scaled = grad_normed_in * gain
    first = lax.optimization_barrier(jnp.mean(scaled, axis=-1, keepdims=True))
    second = lax.optimization_barrier(jnp.mean(scaled * normed, axis=-1, keepdims=True))
    return (scaled - first - normed * second) * inverse

def window_bias(table):
    heads = table.shape[0]
    shaped = table.astype(jnp.float32).reshape(heads, WZ, WZ, WLAT, WLAT, 2 * WLON - 1)
    column = jnp.arange(WLON, dtype=jnp.int32)
    offset = column[:, None] - column[None, :] + (WLON - 1)
    picked = jnp.take(shaped, offset, axis=5)
    picked = picked.transpose(0, 1, 3, 5, 2, 4, 6)
    return picked.reshape(heads, WZ, WLAT, WLON, WZ * WLAT * WLON)

def split_windows(array):
    levels, rows, width, chans = array.shape
    shaped = array.reshape(levels, rows // WLAT, WLAT, width, chans).transpose(1, 0, 2, 3, 4)
    return shaped.reshape(rows // WLAT, levels * WLAT * width, chans)

def join_windows(array, levels, width):
    windows = array.shape[0]
    chans = array.shape[-1]
    shaped = array.reshape(windows, levels, WLAT, width, chans).transpose(1, 0, 2, 3, 4)
    return shaped.reshape(levels, windows * WLAT, width, chans)

def pair_mask(row_start, rows, total_rows, width):
    line = row_start + jnp.arange(rows, dtype=jnp.int32)
    upper = (line >= total_rows - WLAT // 2).reshape(rows // WLAT, 1, WLAT, 1)
    query_side = jnp.broadcast_to(upper, (rows // WLAT, WZ, WLAT, width)).reshape(rows // WLAT, -1)
    key_side = jnp.broadcast_to(upper, (rows // WLAT, WZ, WLAT, 2 * width)).reshape(rows // WLAT, -1)
    return query_side[:, :, None] == key_side[:, None, :]

def attend(queries, keys, values, bias, allowed):
    scale = queries.shape[-1] ** (-0.5)
    scores = jnp.einsum('wqhe,wkhe->whqk', queries.astype(jnp.float32), keys.astype(jnp.float32), precision=highest) * scale + bias
    if allowed is not None:
        scores = jnp.where(allowed[:, None], scores, -1000000000.0)
    largest = lax.optimization_barrier(jnp.max(scores, axis=-1, keepdims=True))
    expo = jnp.exp(scores - largest)
    probs = expo / lax.optimization_barrier(jnp.sum(expo, axis=-1, keepdims=True))
    rounded = lax.optimization_barrier(probs.astype(jnp.bfloat16)).astype(jnp.float32)
    mixed = jnp.einsum('whqk,wkhe->wqhe', rounded, values.astype(jnp.float32), precision=highest)
    return (mixed.astype(jnp.bfloat16), probs)

def attend_back(queries, keys, values, probs, grad_mixed):
    scale = queries.shape[-1] ** (-0.5)
    rounded = lax.optimization_barrier(probs.astype(jnp.bfloat16)).astype(jnp.float32)
    grad_wide = grad_mixed.astype(jnp.float32)
    grad_probs = jnp.einsum('wqhe,wkhe->whqk', grad_wide, values.astype(jnp.float32), precision=highest)
    inner = lax.optimization_barrier(jnp.sum(probs * grad_probs, axis=-1, keepdims=True))
    grad_scores = probs * (grad_probs - inner) * scale
    grad_scores = lax.optimization_barrier(grad_scores.astype(jnp.bfloat16)).astype(jnp.float32)
    grad_q = jnp.einsum('whqk,wkhe->wqhe', grad_scores, keys.astype(jnp.float32), precision=highest)
    grad_k = jnp.einsum('whqk,wqhe->wkhe', grad_scores, queries.astype(jnp.float32), precision=highest)
    grad_v = jnp.einsum('whqk,wqhe->wkhe', rounded, grad_wide, precision=highest)
    return (grad_q, grad_k.astype(jnp.bfloat16), grad_v.astype(jnp.bfloat16))

def column_forward(column, gain, weight_qkv, weight_proj, biases, allowed):
    levels, rows, width, dims = column.shape
    heads = biases.shape[1]
    depth = dims // heads
    windows = rows // WLAT
    half = width // 2
    normed_in, normed, inverse = layer_norm(column, gain)
    projected = jnp.dot(normed_in.reshape(-1, dims), weight_qkv, preferred_element_type=jnp.float32)
    projected = projected.astype(jnp.bfloat16).reshape(levels, rows, width, 3 * dims)
    key_values = split_windows(projected[..., dims:])
    keys = key_values[..., :dims].reshape(windows, -1, heads, depth)
    values = key_values[..., dims:].reshape(windows, -1, heads, depth)
    pieces = []
    saved = []
    for side in range(2):
        queries = split_windows(projected[:, :, side * half:(side + 1) * half, :dims]).reshape(windows, -1, heads, depth)
        bias = biases[:, :, :, :, side * half:(side + 1) * half].reshape(windows, heads, -1, biases.shape[-1])
        mixed, probs = attend(queries, keys, values, bias, allowed)
        pieces.append(join_windows(mixed.reshape(windows, -1, dims), levels, half))
        saved.append((queries, probs))
    mixed_all = jnp.concatenate(pieces, axis=2)
    added = jnp.dot(mixed_all.reshape(-1, dims), weight_proj, preferred_element_type=jnp.float32).reshape(column.shape)
    result = (column.astype(jnp.float32) + added).astype(jnp.bfloat16)
    return (result, (normed, inverse, keys, values, saved))

def column_backward(column, grad, gain, weight_qkv, weight_proj, biases, allowed):
    result, (normed, inverse, keys, values, saved) = column_forward(column, gain, weight_qkv, weight_proj, biases, allowed)
    levels, rows, width, dims = column.shape
    heads = biases.shape[1]
    depth = dims // heads
    windows = rows // WLAT
    half = width // 2
    grad_mixed = jnp.dot(grad.reshape(-1, dims), weight_proj.T, preferred_element_type=jnp.float32)
    grad_mixed = grad_mixed.astype(jnp.bfloat16).reshape(grad.shape)
    query_parts = []
    key_total = jnp.zeros((windows, WZ * WLAT * width, heads, depth), jnp.float32)
    value_total = jnp.zeros((windows, WZ * WLAT * width, heads, depth), jnp.float32)
    for side in range(2):
        queries, probs = saved[side]
        grad_part = split_windows(grad_mixed[:, :, side * half:(side + 1) * half]).reshape(windows, -1, heads, depth)
        grad_q, grad_k, grad_v = attend_back(queries, keys, values, probs, grad_part)
        query_parts.append(join_windows(grad_q.reshape(windows, -1, dims), levels, half))
        key_total = key_total + grad_k.astype(jnp.float32)
        value_total = value_total + grad_v.astype(jnp.float32)
    query_grads = jnp.concatenate(query_parts, axis=2).astype(jnp.bfloat16)
    both = jnp.concatenate([key_total.reshape(windows, -1, dims), value_total.reshape(windows, -1, dims)], axis=-1)
    key_grads = join_windows(both.astype(jnp.bfloat16), levels, width)
    grad_qkv = jnp.concatenate([query_grads, key_grads], axis=-1)
    grad_normed_in = jnp.dot(grad_qkv.reshape(-1, 3 * dims), weight_qkv.T, preferred_element_type=jnp.float32).reshape(grad.shape)
    return (grad.astype(jnp.float32) + norm_back(grad_normed_in, normed, inverse, gain)).astype(jnp.bfloat16)

def run_block(field, gain, weight_qkv, weight_proj, table, allowed, grad):
    levels, rows, width, dims = field.shape
    columns = width // WLON
    biases = jax.vmap(window_bias)(table)
    pieces = field.reshape(levels, rows, columns, WLON, dims).transpose(2, 0, 1, 3, 4)
    if grad is None:

        def forward_one(column):
            return column_forward(column, gain, weight_qkv, weight_proj, biases, allowed)[0]
        done = lax.map(forward_one, pieces)
    else:
        grad_pieces = grad.reshape(levels, rows, columns, WLON, dims).transpose(2, 0, 1, 3, 4)

        def backward_one(pair):
            return column_backward(pair[0], pair[1], gain, weight_qkv, weight_proj, biases, allowed)
        done = lax.map(backward_one, (pieces, grad_pieces))
    return done.transpose(1, 2, 0, 3, 4).reshape(field.shape)

def reference(stream, land, orography, land_vector, orography_table, gain_one, qkv_one, proj_one, table_one, gain_two, qkv_two, proj_two, table_two, cotangent):
    dims = stream.shape[-1]
    onehot = (orography[..., None] == jnp.arange(OROG, dtype=jnp.int32)).astype(jnp.float32)
    looked = jnp.dot(onehot.reshape(-1, OROG), orography_table, precision=highest).reshape(LAT, LON, dims)
    added = (land.astype(jnp.float32) / LAND)[..., None] * land_vector + looked
    embedded = (stream.astype(jnp.float32) + added[None]).astype(jnp.bfloat16)
    shifted = pair_mask(0, LAT, LAT, WLON // 2)
    back_shift = (-(WLAT // 2), -(WLON // 2))
    forth_shift = (WLAT // 2, WLON // 2)
    middle = run_block(embedded, gain_one, qkv_one, proj_one, table_one, None, None)
    rolled = jnp.roll(middle, back_shift, axis=(1, 2))
    turned = run_block(rolled, gain_two, qkv_two, proj_two, table_two, shifted, None)
    output = jnp.roll(turned, forth_shift, axis=(1, 2))
    grad_rolled = jnp.roll(cotangent, back_shift, axis=(1, 2))
    grad_turned = run_block(rolled, gain_two, qkv_two, proj_two, table_two, shifted, grad_rolled)
    grad_middle = jnp.roll(grad_turned, forth_shift, axis=(1, 2))
    grad_stream = run_block(embedded, gain_one, qkv_one, proj_one, table_one, None, grad_middle)
    return (output, grad_stream)
```

```python
import jax
import jax.numpy as jnp
from jax import lax
from jax.experimental import pallas as pl
from jax.experimental.pallas import tpu as pltpu
from jax.sharding import PartitionSpec as P

D = 768
HEADS = 12
DEPTH = 64
TOKENS = 144
HALF = 72
QUAD = 36
CHUNK = 132
OROG = 8
LAND = 16
EPS = 1e-05
LIMIT = 40 * 1024 * 1024

f32 = jnp.float32
bf16 = jnp.bfloat16


def iota(shape, dim):
    return lax.broadcasted_iota(jnp.int32, shape, dim)


def div(a, b):
    return lax.div(a, jnp.int32(b))


def rem(a, b):
    return lax.rem(a, jnp.int32(b))


def dot(a, b):
    return jnp.dot(a, b, preferred_element_type=f32)


def dot_t(a, b):
    return lax.dot_general(a, b, (((1,), (1,)), ((), ())), preferred_element_type=f32)


def t_dot(a, b):
    return lax.dot_general(a, b, (((0,), (0,)), ((), ())), preferred_element_type=f32)


def parity():
    return rem(lax.axis_index("lon").astype(jnp.int32), 2)


def split_token(i):
    level = rem(div(i, 18), 2)
    row = rem(div(i, 36), 2) * 6 + rem(i, 6)
    col = div(i, 72) * 3 + rem(div(i, 6), 3)
    return level, row, col


def natural_place(i, band):
    level = rem(div(i, 18), 2)
    row = band * 12 + div(i, 36) * 6 + rem(i, 6)
    col = rem(div(i, 6), 3)
    return level * 72 + col * 24 + row


def pack_kernel(stream, land, orography, land_vector, orog_table, cotangent, keep, send):
    c = parity()
    kinds = iota((OROG, 24), 0)
    added = []
    for w in range(3):
        onehot = (orography[w : w + 1, :] == kinds).astype(f32)
        looked = lax.dot_general(
            onehot,
            orog_table[...],
            (((0,), (0,)), ((), ())),
            precision=lax.Precision.HIGHEST,
            preferred_element_type=f32,
        )
        share = land[w : w + 1, :].astype(f32) * (1.0 / LAND)
        spread = lax.dot_general(
            jnp.concatenate([share, jnp.zeros((7, 24), f32)], axis=0),
            jnp.concatenate([land_vector[...], jnp.zeros((7, D), f32)], axis=0),
            (((0,), (0,)), ((), ())),
            precision=lax.Precision.HIGHEST,
            preferred_element_type=f32,
        )
        added.append(spread + looked)
    added = jnp.concatenate(added + added, axis=0)
    embedded = (stream[...].astype(f32) + added).astype(bf16)
    out = iota((TOKENS, TOKENS), 0)
    own = out < HALF
    place = natural_place(jnp.where(own, out, out - HALF), jnp.where(own, c, 1 - c))
    move = (iota((TOKENS, TOKENS), 1) == place).astype(f32).astype(bf16)
    e = dot(move, embedded)
    g = dot(move, cotangent[...])
    keep[...] = jnp.concatenate([e[:HALF], g[:HALF]], axis=0).astype(bf16)
    send[...] = jnp.concatenate([e[HALF:], g[HALF:]], axis=0).astype(bf16)


def unpack_kernel(keep, received, output, grad):
    c = parity()
    inp = iota((TOKENS, TOKENS), 1)
    own = inp < HALF
    place = natural_place(jnp.where(own, inp, inp - HALF), jnp.where(own, c, 1 - c))
    move = (iota((TOKENS, TOKENS), 0) == place).astype(f32).astype(bf16)
    k = keep[...].astype(f32)
    r = received[...].astype(f32)
    grads = jnp.concatenate([k[:HALF], r[:HALF]], axis=0).astype(bf16)
    turned = jnp.concatenate([k[HALF:], r[HALF:]], axis=0).astype(bf16)
    grad[...] = dot(move, grads).astype(bf16)
    output[...] = dot(move, turned).astype(bf16)


def bias_kernel(table_one, table_two, bias_one, bias_two, first, second):
    place = iota((TOKENS, TOKENS), 1)
    level, row, col = split_token(iota((TOKENS, TOKENS), 0))
    spread = (place == col * 24 + level * 12 + row).astype(f32).astype(bf16)
    level, row, col = split_token(iota((256, TOKENS), 1))
    lane = iota((256, TOKENS), 0)
    lane = jnp.where(lane < 128, lane, jnp.where(lane < 252, -1000, lane - 124))
    base = lane - row * 11 + col - 5
    picks = []
    for i in range(6):
        hit = base == i
        picks.append(
            [(hit & (level == z)).astype(f32).astype(bf16) for z in range(2)]
        )
    last = (lax.axis_index("lat") == 1) & (parity() == 1)
    half_q = rem(div(iota((TOKENS, TOKENS), 0), QUAD), 2)
    half_k = rem(div(iota((TOKENS, TOKENS), 1), QUAD), 2)
    forbidden = (half_q != half_k) & last
    for table, bias, masked in ((table_one, bias_one, False), (table_two, bias_two, True)):
        for za in range(2):
            for zc in range(2):
                into = second if zc else first
                for ra in range(12):
                    at = ((za * 2 + zc) * 12 + ra) * CHUNK
                    for part, skip in enumerate((0, CHUNK - 128)):
                        into[part, pl.ds(za * 12 + ra, HEADS, stride=24), :] = table[
                            :, at + skip : at + skip + 128
                        ].astype(f32)
        low = jnp.concatenate([first[0], first[1]], axis=1).astype(bf16)
        high = jnp.concatenate([second[0], second[1]], axis=1).astype(bf16)
        parts = [dot(low, picks[i][0]) + dot(high, picks[i][1]) for i in range(6)]
        for n in range(HEADS):
            stacked = jnp.concatenate([part[n * 24 : n * 24 + 24] for part in parts], axis=0)
            one = dot(spread, stacked.astype(bf16))
            if masked:
                one = jnp.where(forbidden, -1e9, one)
            bias[n] = one.astype(bf16)


def norm(u):
    average = jnp.mean(u, axis=-1, keepdims=True)
    centred = u - average
    inverse = lax.rsqrt(jnp.mean(centred * centred, axis=-1, keepdims=True) + EPS)
    return centred * inverse, inverse


def lane_masks(value):
    low = iota((1, 2 * DEPTH), 1) < DEPTH
    return (
        jnp.where(low, value, 0.0).astype(bf16),
        jnp.where(low, 0.0, value).astype(bf16),
    )


def attend(qkv, bias, probs, mixed):
    masks = lane_masks(DEPTH ** (-0.5))
    low = iota((TOKENS, 2 * DEPTH), 1) < DEPTH
    for pair in range(HEADS // 2):
        at = pair * 2 * DEPTH
        q2 = qkv[:, at : at + 128]
        k2 = qkv[:, D + at : D + at + 128]
        v2 = qkv[:, 2 * D + at : 2 * D + at + 128]
        mixes = []
        for side in range(2):
            n = pair * 2 + side
            scores = dot_t(q2 * masks[side], k2) + bias[n].astype(f32)
            expo = jnp.exp(scores - jnp.max(scores, axis=-1, keepdims=True))
            p = (expo * (1.0 / jnp.sum(expo, axis=-1, keepdims=True))).astype(bf16)
            probs[n] = p
            mixes.append(dot(p, v2))
        mixed[:, at : at + 128] = jnp.where(low, mixes[0], mixes[1]).astype(bf16)


def attend_back(qkv, probs, grad_mixed, grad_qkv):
    masks = lane_masks(1.0)
    low = iota((TOKENS, 2 * DEPTH), 1) < DEPTH
    for pair in range(HEADS // 2):
        at = pair * 2 * DEPTH
        q2 = qkv[:, at : at + 128]
        k2 = qkv[:, D + at : D + at + 128]
        v2 = qkv[:, 2 * D + at : 2 * D + at + 128]
        g2 = grad_mixed[:, at : at + 128]
        dq, dk, dv = [], [], []
        for side in range(2):
            n = pair * 2 + side
            p = probs[n]
            pf = p.astype(f32)
            dp = dot_t(g2 * masks[side], v2)
            inner = jnp.sum(pf * dp, axis=-1, keepdims=True)
            ds = (pf * (dp - inner) * (DEPTH ** (-0.5))).astype(bf16)
            dq.append(dot(ds, k2))
            dk.append(t_dot(ds, q2))
            dv.append(t_dot(p, g2))
        for block, part in enumerate((dq, dk, dv)):
            grad_qkv[:, block * D + at : block * D + at + 128] = jnp.where(
                low, part[0], part[1]
            ).astype(bf16)


def norm_back(dh, gain, normed, inverse):
    dn = dh * gain
    first = jnp.mean(dn, axis=-1, keepdims=True)
    second = jnp.mean(dn * normed, axis=-1, keepdims=True)
    return (dn - first - normed * second) * inverse


def piece(array, index):
    return array[index * QUAD : (index + 1) * QUAD]


def one_kernel(
    keep, received, gain, weight_qkv, weight_proj, bias,
    stay, left, up, corner, u_out, qkv, probs, mixed,
):
    c = parity()
    k = keep[...].astype(f32)
    r = received[...].astype(f32)
    mine = c == 0
    lead = jnp.where(mine, k, r)
    trail = jnp.where(mine, r, k)
    u = jnp.concatenate([lead[:HALF], trail[:HALF]], axis=0)
    g = jnp.concatenate([lead[HALF:], trail[HALF:]], axis=0)
    u_out[...] = u.astype(bf16)
    normed, _ = norm(u)
    h = (normed * gain[...]).astype(bf16)
    qkv[...] = dot(h, weight_qkv[...]).astype(bf16)
    attend(qkv, bias, probs, mixed)
    middle = u + dot(mixed[...], weight_proj[...])
    for index, out in ((0, corner), (1, left), (2, up), (3, stay)):
        out[...] = jnp.concatenate([piece(middle, index), piece(g, index)], axis=0).astype(bf16)


def two_kernel(
    stay, right, down, corner, gain, weight_qkv, weight_proj, bias,
    back_stay, back_right, back_down, back_corner,
    qkv, probs, mixed, grad_mixed, grad_qkv,
):
    parts = [ref[...].astype(f32) for ref in (stay, down, right, corner)]
    u = jnp.concatenate([part[:QUAD] for part in parts], axis=0)
    g = jnp.concatenate([part[QUAD:] for part in parts], axis=0)
    normed, inverse = norm(u)
    h = (normed * gain[...]).astype(bf16)
    qkv[...] = dot(h, weight_qkv[...]).astype(bf16)
    attend(qkv, bias, probs, mixed)
    turned = u + dot(mixed[...], weight_proj[...])
    grad_mixed[...] = dot_t(g.astype(bf16), weight_proj[...]).astype(bf16)
    attend_back(qkv, probs, grad_mixed, grad_qkv)
    dh = dot_t(grad_qkv[...], weight_qkv[...])
    du = g + norm_back(dh, gain[...], normed, inverse)
    for index, out in ((0, back_stay), (1, back_down), (2, back_right), (3, back_corner)):
        out[...] = jnp.concatenate([piece(du, index), piece(turned, index)], axis=0).astype(bf16)


def three_kernel(
    stay, left, up, corner, u, qkv, probs, gain, weight_qkv, weight_proj,
    keep, send, grad_mixed, grad_qkv,
):
    c = parity()
    parts = [ref[...].astype(f32) for ref in (corner, left, up, stay)]
    g = jnp.concatenate([part[:QUAD] for part in parts], axis=0)
    turned = jnp.concatenate([part[QUAD:] for part in parts], axis=0)
    normed, inverse = norm(u[...].astype(f32))
    grad_mixed[...] = dot_t(g.astype(bf16), weight_proj[...]).astype(bf16)
    attend_back(qkv, probs, grad_mixed, grad_qkv)
    dh = dot_t(grad_qkv[...], weight_qkv[...])
    du = g + norm_back(dh, gain[...], normed, inverse)
    mine = c == 0
    first = jnp.concatenate([du[:HALF], turned[:HALF]], axis=0)
    second = jnp.concatenate([du[HALF:], turned[HALF:]], axis=0)
    keep[...] = jnp.where(mine, first, second).astype(bf16)
    send[...] = jnp.where(mine, second, first).astype(bf16)


def shape(*dims, dtype=bf16):
    return jax.ShapeDtypeStruct(dims, dtype)


def call(kernel, outs, scratch, *args):
    return pl.pallas_call(
        kernel,
        out_shape=outs,
        scratch_shapes=scratch,
        compiler_params=pltpu.CompilerParams(vmem_limit_bytes=LIMIT),
    )(*args)


def moved(value, lat_size, lon_size, dt, dp):
    bands, columns = 2 * lat_size, lon_size // 2

    def device(t, p):
        return t // 2 * lon_size + 2 * p + t % 2

    pairs = [
        (device(t, p), device((t + dt) % bands, (p + dp) % columns))
        for t in range(bands)
        for p in range(columns)
    ]
    return lax.ppermute(value, ("lat", "lon"), pairs)


def body(
    stream, land, orography, land_vector, orography_table,
    gain_one, qkv_one, proj_one, table_one,
    gain_two, qkv_two, proj_two, table_two, cotangent,
):
    lats = lax.axis_size("lat")
    lons = lax.axis_size("lon")
    swap = [(i, i ^ 1) for i in range(lons)]
    c = lax.axis_index("lon") % 2

    def flat(array):
        return array.transpose(0, 2, 1, 3).reshape(TOKENS, D)

    def field(array):
        return array.reshape(2, 3, 24, D).transpose(0, 2, 1, 3)

    tokens = shape(TOKENS, D)
    quad = shape(2 * QUAD, D)
    keep, send = call(
        pack_kernel, (tokens, tokens), [],
        flat(stream), land.T, orography.T, land_vector[None], orography_table, flat(cotangent),
    )
    received = lax.ppermute(send, "lon", swap)
    bias_shape = shape(HEADS, TOKENS, TOKENS)
    bias_one, bias_two = call(
        bias_kernel, (bias_shape, bias_shape), [pltpu.VMEM((2, HEADS * 24, 128), f32)] * 2,
        lax.dynamic_index_in_dim(table_one, c, 0, False),
        lax.dynamic_index_in_dim(table_two, c, 0, False),
    )
    wide = pltpu.VMEM((TOKENS, 3 * D), bf16)
    narrow = pltpu.VMEM((TOKENS, D), bf16)
    square = pltpu.VMEM((HEADS, TOKENS, TOKENS), bf16)
    stay, left, up, corner, u_one, saved_qkv, saved_probs = call(
        one_kernel,
        (quad, quad, quad, quad, tokens, shape(TOKENS, 3 * D), bias_shape),
        [narrow],
        keep, received, gain_one[None], qkv_one, proj_one, bias_one,
    )
    right = moved(left, lats, lons, 0, -1)
    down = moved(up, lats, lons, -1, 0)
    corner = moved(corner, lats, lons, -1, -1)
    stay, right, down, corner = call(
        two_kernel, (quad, quad, quad, quad), [wide, square, narrow, narrow, wide],
        stay, right, down, corner, gain_two[None], qkv_two, proj_two, bias_two,
    )
    left = moved(right, lats, lons, 0, 1)
    up = moved(down, lats, lons, 1, 0)
    corner = moved(corner, lats, lons, 1, 1)
    keep, send = call(
        three_kernel, (tokens, tokens), [narrow, wide],
        stay, left, up, corner, u_one, saved_qkv, saved_probs, gain_one[None], qkv_one, proj_one,
    )
    received = lax.ppermute(send, "lon", swap)
    output, grad = call(unpack_kernel, (tokens, tokens), [], keep, received)
    return field(output), field(grad)


def solution(mesh):
    tokens = P(None, "lat", "lon", None)
    table = P("lat", None, None)
    placed = (
        tokens, P("lat", "lon"), P("lat", "lon"), P(), P(),
        P(), P(), P(), table, P(), P(), P(), table, tokens,
    )
    return jax.shard_map(
        body, mesh=mesh, in_specs=placed, out_specs=(tokens, tokens), check_vma=False
    )
```

```python
import functools

import jax
import jax.numpy as jnp
from jax import lax
from jax.experimental import pallas as pl
from jax.experimental.pallas import tpu as pltpu
from jax.sharding import PartitionSpec as P

D = 768
HEADS = 12
DEPTH = 64
TOKENS = 144
HALF = 72
QUAD = 36
CHUNK = 132
OROG = 8
LAND = 16
EPS = 1e-05

f32 = jnp.float32
bf16 = jnp.bfloat16


def iota(shape, dim):
    return lax.broadcasted_iota(jnp.int32, shape, dim)


def div(a, b):
    return lax.div(a, jnp.int32(b))


def rem(a, b):
    return lax.rem(a, jnp.int32(b))


def dot(a, b):
    return jnp.dot(a, b, preferred_element_type=f32)


def dot_t(a, b):
    return lax.dot_general(a, b, (((1,), (1,)), ((), ())), preferred_element_type=f32)


def t_dot(a, b):
    return lax.dot_general(a, b, (((0,), (0,)), ((), ())), preferred_element_type=f32)


def parity():
    return rem(lax.axis_index("lon").astype(jnp.int32), 2)


def split_token(i):
    level = rem(div(i, 18), 2)
    line = rem(div(i, 36), 2) * 6 + rem(i, 6)
    col = div(i, 72) * 3 + rem(div(i, 6), 3)
    return level, line, col


def natural_place(i, band):
    level = rem(div(i, 18), 2)
    row = band * 12 + div(i, 36) * 6 + rem(i, 6)
    col = rem(div(i, 6), 3)
    return level * 72 + col * 24 + row


def pack_kernel(
    stream_at, land_at, orography_at, vector_at, table_at, cotangent_at, keep, send,
    stream, land, orography, land_vector, orog_table, cotangent, sems,
):
    c = parity()
    copies = [
        pltpu.make_async_copy(source, target, sems.at[index])
        for index, (source, target) in enumerate((
            (stream_at, stream), (cotangent_at, cotangent), (table_at, orog_table),
            (vector_at, land_vector), (land_at, land), (orography_at, orography),
        ))
    ]
    for copy in copies:
        copy.start()
    out = iota((TOKENS, TOKENS), 0)
    own = out < HALF
    place = natural_place(jnp.where(own, out, out - HALF), jnp.where(own, c, 1 - c))
    move = (iota((TOKENS, TOKENS), 1) == place).astype(f32).astype(bf16)
    for copy in copies:
        copy.wait()
    kinds = iota((OROG, 24), 0)
    added = []
    for w in range(3):
        onehot = (orography[w : w + 1, :] == kinds).astype(f32)
        looked = lax.dot_general(
            onehot,
            orog_table[...],
            (((0,), (0,)), ((), ())),
            precision=lax.Precision.HIGHEST,
            preferred_element_type=f32,
        )
        share = land[w : w + 1, :].astype(f32) * (1.0 / LAND)
        spread = lax.dot_general(
            jnp.concatenate([share, jnp.zeros((7, 24), f32)], axis=0),
            jnp.concatenate([row(land_vector), jnp.zeros((7, D), f32)], axis=0),
            (((0,), (0,)), ((), ())),
            precision=lax.Precision.HIGHEST,
            preferred_element_type=f32,
        )
        added.append(spread + looked)
    added = jnp.concatenate(added + added, axis=0)
    embedded = (stream[...].astype(f32) + added).astype(bf16)
    e = dot(move, embedded)
    g = dot(move, cotangent[...])
    keep[...] = jnp.concatenate([e[:HALF], g[:HALF]], axis=0).astype(bf16)
    send[...] = jnp.concatenate([e[HALF:], g[HALF:]], axis=0).astype(bf16)


def unpack_kernel(keep, received, output, grad):
    c = parity()
    inp = iota((TOKENS, TOKENS), 1)
    own = inp < HALF
    place = natural_place(jnp.where(own, inp, inp - HALF), jnp.where(own, c, 1 - c))
    move = (iota((TOKENS, TOKENS), 0) == place).astype(f32).astype(bf16)
    k = keep[...].astype(f32)
    r = received[...].astype(f32)
    grads = jnp.concatenate([k[:HALF], r[:HALF]], axis=0).astype(bf16)
    turned = jnp.concatenate([k[HALF:], r[HALF:]], axis=0).astype(bf16)
    grad[...] = dot(move, grads).astype(bf16)
    output[...] = dot(move, turned).astype(bf16)


def bias_kernel(masked, table, bias, first, second):
    place = iota((TOKENS, TOKENS), 1)
    level, line, col = split_token(iota((TOKENS, TOKENS), 0))
    spread = (place == col * 24 + level * 12 + line).astype(f32).astype(bf16)
    level, line, col = split_token(iota((256, TOKENS), 1))
    lane = iota((256, TOKENS), 0)
    lane = jnp.where(lane < 128, lane, jnp.where(lane < 252, -1000, lane - 124))
    base = lane - line * 11 + col - 5
    for za in range(2):
        for zc in range(2):
            into = second if zc else first
            for ra in range(12):
                at = ((za * 2 + zc) * 12 + ra) * CHUNK
                for part, skip in enumerate((0, CHUNK - 128)):
                    into[part, pl.ds(za * 12 + ra, HEADS, stride=24), :] = table[
                        :, at + skip : at + skip + 128
                    ].astype(f32)
    low = jnp.concatenate([first[0], first[1]], axis=1).astype(bf16)
    high = jnp.concatenate([second[0], second[1]], axis=1).astype(bf16)
    parts = []
    for i in range(6):
        hit = base == i
        pick_low = (hit & (level == 0)).astype(f32).astype(bf16)
        pick_high = (hit & (level == 1)).astype(f32).astype(bf16)
        parts.append(dot(low, pick_low) + dot(high, pick_high))
    if masked:
        last = (lax.axis_index("lat") == lax.axis_size("lat") - 1) & (parity() == 1)
        half_q = rem(div(iota((TOKENS, TOKENS), 0), QUAD), 2)
        half_k = rem(div(iota((TOKENS, TOKENS), 1), QUAD), 2)
        forbidden = (half_q != half_k) & last
    for n in range(HEADS):
        stacked = jnp.concatenate([part[n * 24 : n * 24 + 24] for part in parts], axis=0)
        one = dot(spread, stacked.astype(bf16))
        if masked:
            one = jnp.where(forbidden, -1e9, one)
        bias[n] = one.astype(bf16).T


def norm(u):
    average = jnp.mean(u, axis=-1, keepdims=True)
    centred = u - average
    inverse = lax.rsqrt(jnp.mean(centred * centred, axis=-1, keepdims=True) + EPS)
    return centred * inverse, inverse


def row(vector):
    return vector[...].reshape(1, D)


def lane_masks(value):
    low = iota((1, 2 * DEPTH), 1) < DEPTH
    return (
        jnp.where(low, value, 0.0).astype(bf16),
        jnp.where(low, 0.0, value).astype(bf16),
    )


def attend(qkv, bias, probs, mixed):
    masks = lane_masks(DEPTH ** (-0.5))
    low = iota((TOKENS, 2 * DEPTH), 1) < DEPTH
    for pair in range(HEADS // 2):
        at = pair * 2 * DEPTH
        q2 = qkv[:, at : at + 128]
        k2 = qkv[:, D + at : D + at + 128]
        v2 = qkv[:, 2 * D + at : 2 * D + at + 128]
        both = dot_t(jnp.concatenate([k2 * masks[0], k2 * masks[1]], axis=0), q2)
        turned = []
        for side in range(2):
            n = pair * 2 + side
            scores = both[side * TOKENS : side * TOKENS + TOKENS] + bias[n].astype(f32)
            expo = jnp.exp(scores - jnp.max(scores, axis=0, keepdims=True))
            p = (expo * (1.0 / jnp.sum(expo, axis=0, keepdims=True))).astype(bf16)
            probs[n] = p
            turned.append(p.T)
        both = dot(jnp.concatenate(turned, axis=0), v2)
        mixed[:, at : at + 128] = jnp.where(low, both[:TOKENS], both[TOKENS:]).astype(bf16)


def attend_back(qkv, probs, grad_mixed, grad_qkv):
    masks = lane_masks(1.0)
    low = iota((TOKENS, 2 * DEPTH), 1) < DEPTH
    for pair in range(HEADS // 2):
        at = pair * 2 * DEPTH
        q2 = qkv[:, at : at + 128]
        k2 = qkv[:, D + at : D + at + 128]
        v2 = qkv[:, 2 * D + at : 2 * D + at + 128]
        g2 = grad_mixed[:, at : at + 128]
        both = dot_t(jnp.concatenate([v2 * masks[0], v2 * masks[1]], axis=0), g2)
        ps, ds, ds_t = [], [], []
        for side in range(2):
            p = probs[pair * 2 + side]
            wide = p.astype(f32)
            dp = both[side * TOKENS : side * TOKENS + TOKENS]
            inner = jnp.sum(wide * dp, axis=0, keepdims=True)
            d = (wide * (dp - inner) * (DEPTH ** (-0.5))).astype(bf16)
            ps.append(p)
            ds.append(d)
            ds_t.append(d.T)
        for block, (lhs, rhs) in enumerate(((ds_t, k2), (ds, q2), (ps, g2))):
            both = dot(jnp.concatenate(lhs, axis=0), rhs)
            grad_qkv[:, block * D + at : block * D + at + 128] = jnp.where(
                low, both[:TOKENS], both[TOKENS:]
            ).astype(bf16)


def norm_back(dh, gain, normed, inverse):
    dn = dh * gain
    first = jnp.mean(dn, axis=-1, keepdims=True)
    second = jnp.mean(dn * normed, axis=-1, keepdims=True)
    return (dn - first - normed * second) * inverse


def pieces(array):
    return [array[index * QUAD : (index + 1) * QUAD] for index in range(4)]


QUARTERS_ONE = ((3, 1), (1, 3), (0, 2), (2, 0))
QUARTERS_TWO = ((0, 2), (2, 0), (1, 3), (3, 1))


def deal(quarters, c, refs, above, below):
    tops, bottoms = pieces(above), pieces(below)
    even = c == 0
    for (first, second), out in zip(quarters, refs):
        out[...] = jnp.concatenate(
            [jnp.where(even, part[first], part[second]) for part in (tops, bottoms)], axis=0
        ).astype(bf16)


def gather(quarters, c, refs):
    even = c == 0
    values = [ref[...].astype(f32) for ref in refs]
    chosen = []
    for index in range(4):
        at_even = [first for first, _ in quarters].index(index)
        at_odd = [second for _, second in quarters].index(index)
        chosen.append(jnp.where(even, values[at_even], values[at_odd]))
    return (
        jnp.concatenate([value[:QUAD] for value in chosen], axis=0),
        jnp.concatenate([value[QUAD:] for value in chosen], axis=0),
    )


def one_kernel(
    keep, received, gain, weight_qkv, weight_proj, bias,
    stay, first, second, third, u_out, qkv, probs, mixed,
):
    c = parity()
    k = keep[...].astype(f32)
    r = received[...].astype(f32)
    mine = c == 0
    lead = jnp.where(mine, k, r)
    trail = jnp.where(mine, r, k)
    u = jnp.concatenate([lead[:HALF], trail[:HALF]], axis=0)
    g = jnp.concatenate([lead[HALF:], trail[HALF:]], axis=0)
    u_out[...] = u.astype(bf16)
    normed, _ = norm(u)
    h = (normed * row(gain)).astype(bf16)
    qkv[...] = dot(h, weight_qkv[...]).astype(bf16)
    attend(qkv, bias, probs, mixed)
    middle = u + dot(mixed[...], weight_proj[...])
    deal(QUARTERS_ONE, c, (stay, first, second, third), middle, g)


def two_kernel(
    stay, first, second, third, gain, weight_qkv, weight_proj, bias,
    back_stay, back_first, back_second, back_third,
    qkv, probs, mixed, grad_mixed, grad_qkv,
):
    c = parity()
    u, g = gather(QUARTERS_TWO, c, (stay, first, second, third))
    normed, inverse = norm(u)
    h = (normed * row(gain)).astype(bf16)
    qkv[...] = dot(h, weight_qkv[...]).astype(bf16)
    attend(qkv, bias, probs, mixed)
    turned = u + dot(mixed[...], weight_proj[...])
    grad_mixed[...] = dot_t(g.astype(bf16), weight_proj[...]).astype(bf16)
    attend_back(qkv, probs, grad_mixed, grad_qkv)
    dh = dot_t(grad_qkv[...], weight_qkv[...])
    du = g + norm_back(dh, row(gain), normed, inverse)
    deal(QUARTERS_TWO, c, (back_stay, back_first, back_second, back_third), du, turned)


def three_kernel(
    stay, first, second, third, u, qkv, probs, gain, weight_qkv, weight_proj,
    keep, send, grad_mixed, grad_qkv,
):
    c = parity()
    g, turned = gather(QUARTERS_ONE, c, (stay, first, second, third))
    normed, inverse = norm(u[...].astype(f32))
    grad_mixed[...] = dot_t(g.astype(bf16), weight_proj[...]).astype(bf16)
    attend_back(qkv, probs, grad_mixed, grad_qkv)
    dh = dot_t(grad_qkv[...], weight_qkv[...])
    du = g + norm_back(dh, row(gain), normed, inverse)
    mine = c == 0
    low = jnp.concatenate([du[:HALF], turned[:HALF]], axis=0)
    high = jnp.concatenate([du[HALF:], turned[HALF:]], axis=0)
    keep[...] = jnp.where(mine, low, high).astype(bf16)
    send[...] = jnp.where(mine, high, low).astype(bf16)


def shape(*dims, dtype=bf16):
    return jax.ShapeDtypeStruct(dims, dtype)


def call(kernel, outs, scratch, mib, micros, *args, **options):
    return pl.pallas_call(
        kernel,
        out_shape=outs,
        scratch_shapes=scratch,
        compiler_params=pltpu.CompilerParams(vmem_limit_bytes=mib * 1024 * 1024),
        cost_estimate=pl.CostEstimate(
            flops=int(micros * 1e9), bytes_accessed=int(micros * 3e6), transcendentals=0
        ),
        **options,
    )(*args)


def exchange(number, back):
    lats, lons = lax.axis_size("lat"), lax.axis_size("lon")

    def device(a, p, c):
        return a % lats * lons + 2 * p % lons + c

    pairs = []
    for a in range(lats):
        for p in range(lons // 2):
            even, odd = (
                (device(a, p - 1, 0), device(a, p + 1, 1)),
                (device(a - 1, p, 1), device(a, p, 0)),
                (device(a - 1, p + 1, 1), device(a, p - 1, 0)),
            )[number]
            pairs += [(device(a, p, 0), even), (device(a, p, 1), odd)]
    return [(target, source) for source, target in pairs] if back else pairs


def exchanged(values, back):
    return [
        lax.ppermute(value, ("lat", "lon"), exchange(number, back))
        for number, value in enumerate(values)
    ]


def body(
    stream, land, orography, land_vector, orography_table,
    gain_one, qkv_one, proj_one, table_one,
    gain_two, qkv_two, proj_two, table_two, cotangent,
):
    swap = [(i, i ^ 1) for i in range(lax.axis_size("lon"))]
    c = lax.axis_index("lon") % 2

    def flat(array):
        return array.transpose(0, 2, 1, 3).reshape(TOKENS, D)

    def field(array):
        return array.reshape(2, 3, 24, D).transpose(0, 2, 1, 3)

    tokens = shape(TOKENS, D)
    quad = shape(2 * QUAD, D)
    wide = pltpu.VMEM((TOKENS, 3 * D), bf16)
    narrow = pltpu.VMEM((TOKENS, D), bf16)
    keep, send = call(
        pack_kernel, (tokens, tokens),
        [
            narrow, pltpu.VMEM((3, 24), jnp.int32), pltpu.VMEM((3, 24), jnp.int32),
            pltpu.VMEM((D,), f32), pltpu.VMEM((OROG, D), f32), narrow,
            pltpu.SemaphoreType.DMA((6,)),
        ],
        56, 3.0,
        flat(stream), land.T, orography.T, land_vector, orography_table, flat(cotangent),
        in_specs=[pl.BlockSpec(memory_space=pltpu.HBM)] * 6,
    )
    received = lax.ppermute(send, "lon", swap)
    square = shape(HEADS, TOKENS, TOKENS)

    def bias_of(table, masked):
        return call(
            functools.partial(bias_kernel, masked), square,
            [pltpu.VMEM((2, HEADS * 24, 128), f32)] * 2, 8, 1.5,
            lax.dynamic_index_in_dim(table, c, 0, False),
        )

    stay, *leave, u_one, saved_qkv, saved_probs = call(
        one_kernel,
        (quad, quad, quad, quad, tokens, shape(TOKENS, 3 * D), square),
        [narrow], 16, 3.0,
        keep, received, gain_one, qkv_one, proj_one, bias_of(table_one, False),
    )
    table_two, stay = lax.optimization_barrier((table_two, stay))
    arrived = exchanged(leave, False)
    stay, *leave = call(
        two_kernel, (quad, quad, quad, quad),
        [wide, pltpu.VMEM((HEADS, TOKENS, TOKENS), bf16), narrow, narrow, wide], 16, 8.0,
        stay, *arrived, gain_two, qkv_two, proj_two, bias_of(table_two, True),
    )
    arrived = exchanged(leave, True)
    keep, send = call(
        three_kernel, (tokens, tokens), [narrow, wide], 16, 6.0,
        stay, *arrived, u_one, saved_qkv, saved_probs, gain_one, qkv_one, proj_one,
    )
    received = lax.ppermute(send, "lon", swap)
    output, grad = call(unpack_kernel, (tokens, tokens), [], 8, 1.0, keep, received)
    return field(output), field(grad)


def solution(mesh):
    tokens = P(None, "lat", "lon", None)
    table = P("lat", None, None)
    placed = (
        tokens, P("lat", "lon"), P("lat", "lon"), P(), P(),
        P(), P(), P(), table, P(), P(), P(), table, tokens,
    )
    return jax.shard_map(
        body, mesh=mesh, in_specs=placed, out_specs=(tokens, tokens), check_vma=False
    )
```

```python
import functools

import jax
import jax.numpy as jnp
from jax import lax
from jax.experimental import pallas as pl
from jax.experimental.pallas import tpu as pltpu
from jax.sharding import PartitionSpec as P

D = 768
HEADS = 12
DEPTH = 64
TOKENS = 144
HALF = 72
QUAD = 36
CHUNK = 132
OROG = 8
LAND = 16
EPS = 1e-05

f32 = jnp.float32
bf16 = jnp.bfloat16


def iota(shape, dim):
    return lax.broadcasted_iota(jnp.int32, shape, dim)


def div(a, b):
    return lax.div(a, jnp.int32(b))


def rem(a, b):
    return lax.rem(a, jnp.int32(b))


def dot(a, b):
    return jnp.dot(a, b, preferred_element_type=f32)


def dot_t(a, b):
    return lax.dot_general(a, b, (((1,), (1,)), ((), ())), preferred_element_type=f32)


def t_dot(a, b):
    return lax.dot_general(a, b, (((0,), (0,)), ((), ())), preferred_element_type=f32)


def parity():
    return rem(lax.axis_index("lon").astype(jnp.int32), 2)


def split_token(i):
    level = rem(div(i, 18), 2)
    line = rem(div(i, 36), 2) * 6 + rem(i, 6)
    col = div(i, 72) * 3 + rem(div(i, 6), 3)
    return level, line, col


def natural_place(i, band):
    level = rem(div(i, 18), 2)
    row = band * 12 + div(i, 36) * 6 + rem(i, 6)
    col = rem(div(i, 6), 3)
    return level * 72 + col * 24 + row


def pack_kernel(
    stream_at, land_at, orography_at, vector_at, table_at, cotangent_at, keep, send,
    stream, land, orography, land_vector, orog_table, cotangent, sems,
):
    c = parity()
    copies = [
        pltpu.make_async_copy(source, target, sems.at[index])
        for index, (source, target) in enumerate((
            (stream_at, stream), (cotangent_at, cotangent), (table_at, orog_table),
            (vector_at, land_vector), (land_at, land), (orography_at, orography),
        ))
    ]
    for copy in copies:
        copy.start()
    out = iota((TOKENS, TOKENS), 0)
    own = out < HALF
    place = natural_place(jnp.where(own, out, out - HALF), jnp.where(own, c, 1 - c))
    move = (iota((TOKENS, TOKENS), 1) == place).astype(f32).astype(bf16)
    for copy in copies:
        copy.wait()
    kinds = iota((OROG, 24), 0)
    added = []
    for w in range(3):
        onehot = (orography[w : w + 1, :] == kinds).astype(f32)
        looked = lax.dot_general(
            onehot,
            orog_table[...],
            (((0,), (0,)), ((), ())),
            precision=lax.Precision.HIGHEST,
            preferred_element_type=f32,
        )
        share = land[w : w + 1, :].astype(f32) * (1.0 / LAND)
        spread = lax.dot_general(
            jnp.concatenate([share, jnp.zeros((7, 24), f32)], axis=0),
            jnp.concatenate([row(land_vector), jnp.zeros((7, D), f32)], axis=0),
            (((0,), (0,)), ((), ())),
            precision=lax.Precision.HIGHEST,
            preferred_element_type=f32,
        )
        added.append(spread + looked)
    added = jnp.concatenate(added + added, axis=0)
    embedded = (stream[...].astype(f32) + added).astype(bf16)
    e = dot(move, embedded)
    g = dot(move, cotangent[...])
    keep[...] = jnp.concatenate([e[:HALF], g[:HALF]], axis=0).astype(bf16)
    send[...] = jnp.concatenate([e[HALF:], g[HALF:]], axis=0).astype(bf16)


def unpack_kernel(keep, received, output, grad):
    c = parity()
    inp = iota((TOKENS, TOKENS), 1)
    own = inp < HALF
    place = natural_place(jnp.where(own, inp, inp - HALF), jnp.where(own, c, 1 - c))
    move = (iota((TOKENS, TOKENS), 0) == place).astype(f32).astype(bf16)
    k = keep[...].astype(f32)
    r = received[...].astype(f32)
    grads = jnp.concatenate([k[:HALF], r[:HALF]], axis=0).astype(bf16)
    turned = jnp.concatenate([k[HALF:], r[HALF:]], axis=0).astype(bf16)
    grad[...] = dot(move, grads).astype(bf16)
    output[...] = dot(move, turned).astype(bf16)


def bias_kernel(masked, table, bias, first, second):
    place = iota((TOKENS, TOKENS), 1)
    level, line, col = split_token(iota((TOKENS, TOKENS), 0))
    spread = (place == col * 24 + level * 12 + line).astype(f32).astype(bf16)
    level, line, col = split_token(iota((256, TOKENS), 1))
    lane = iota((256, TOKENS), 0)
    lane = jnp.where(lane < 128, lane, jnp.where(lane < 252, -1000, lane - 124))
    base = lane - line * 11 + col - 5
    for za in range(2):
        for zc in range(2):
            into = second if zc else first
            for ra in range(12):
                at = ((za * 2 + zc) * 12 + ra) * CHUNK
                for part, skip in enumerate((0, CHUNK - 128)):
                    into[part, pl.ds(za * 12 + ra, HEADS, stride=24), :] = table[
                        :, at + skip : at + skip + 128
                    ].astype(f32)
    low = jnp.concatenate([first[0], first[1]], axis=1).astype(bf16)
    high = jnp.concatenate([second[0], second[1]], axis=1).astype(bf16)
    parts = []
    for i in range(6):
        hit = base == i
        pick_low = (hit & (level == 0)).astype(f32).astype(bf16)
        pick_high = (hit & (level == 1)).astype(f32).astype(bf16)
        parts.append(dot(low, pick_low) + dot(high, pick_high))
    if masked:
        last = (lax.axis_index("lat") == lax.axis_size("lat") - 1) & (parity() == 1)
        half_q = rem(div(iota((TOKENS, TOKENS), 0), QUAD), 2)
        half_k = rem(div(iota((TOKENS, TOKENS), 1), QUAD), 2)
        forbidden = (half_q != half_k) & last
    for n in range(HEADS):
        stacked = jnp.concatenate([part[n * 24 : n * 24 + 24] for part in parts], axis=0)
        one = dot(spread, stacked.astype(bf16))
        if masked:
            one = jnp.where(forbidden, -1e9, one)
        bias[n] = one.astype(bf16).T


def norm(u):
    average = jnp.mean(u, axis=-1, keepdims=True)
    centred = u - average
    inverse = lax.rsqrt(jnp.mean(centred * centred, axis=-1, keepdims=True) + EPS)
    return centred * inverse, inverse


def row(vector):
    return vector[...].reshape(1, D)


def lane_masks(value):
    low = iota((1, 2 * DEPTH), 1) < DEPTH
    return (
        jnp.where(low, value, 0.0).astype(bf16),
        jnp.where(low, 0.0, value).astype(bf16),
    )


def attend(qkv, bias, probs, mixed):
    masks = lane_masks(DEPTH ** (-0.5))
    low = iota((TOKENS, 2 * DEPTH), 1) < DEPTH
    for pair in range(HEADS // 2):
        at = pair * 2 * DEPTH
        q2 = qkv[:, at : at + 128]
        k2 = qkv[:, D + at : D + at + 128]
        v2 = qkv[:, 2 * D + at : 2 * D + at + 128]
        both = dot_t(jnp.concatenate([k2 * masks[0], k2 * masks[1]], axis=0), q2)
        turned = []
        for side in range(2):
            n = pair * 2 + side
            scores = both[side * TOKENS : side * TOKENS + TOKENS] + bias[n].astype(f32)
            expo = jnp.exp(scores - jnp.max(scores, axis=0, keepdims=True))
            p = (expo * (1.0 / jnp.sum(expo, axis=0, keepdims=True))).astype(bf16)
            probs[n] = p
            turned.append(p.T)
        both = dot(jnp.concatenate(turned, axis=0), v2)
        mixed[:, at : at + 128] = jnp.where(low, both[:TOKENS], both[TOKENS:]).astype(bf16)


def attend_back(qkv, probs, grad_mixed, grad_qkv):
    masks = lane_masks(1.0)
    low = iota((TOKENS, 2 * DEPTH), 1) < DEPTH
    for pair in range(HEADS // 2):
        at = pair * 2 * DEPTH
        q2 = qkv[:, at : at + 128]
        k2 = qkv[:, D + at : D + at + 128]
        v2 = qkv[:, 2 * D + at : 2 * D + at + 128]
        g2 = grad_mixed[:, at : at + 128]
        both = dot_t(jnp.concatenate([v2 * masks[0], v2 * masks[1]], axis=0), g2)
        ps, ds, ds_t = [], [], []
        for side in range(2):
            p = probs[pair * 2 + side]
            wide = p.astype(f32)
            dp = both[side * TOKENS : side * TOKENS + TOKENS]
            inner = jnp.sum(wide * dp, axis=0, keepdims=True)
            d = (wide * (dp - inner) * (DEPTH ** (-0.5))).astype(bf16)
            ps.append(p)
            ds.append(d)
            ds_t.append(d.T)
        for block, (lhs, rhs) in enumerate(((ds_t, k2), (ds, q2), (ps, g2))):
            both = dot(jnp.concatenate(lhs, axis=0), rhs)
            grad_qkv[:, block * D + at : block * D + at + 128] = jnp.where(
                low, both[:TOKENS], both[TOKENS:]
            ).astype(bf16)


def norm_back(dh, gain, normed, inverse):
    dn = dh * gain
    first = jnp.mean(dn, axis=-1, keepdims=True)
    second = jnp.mean(dn * normed, axis=-1, keepdims=True)
    return (dn - first - normed * second) * inverse


def pieces(array):
    return [array[index * QUAD : (index + 1) * QUAD] for index in range(4)]


QUARTERS_ONE = ((1, 3), (3, 1), (2, 0), (0, 2))
QUARTERS_TWO = ((2, 0), (0, 2), (3, 1), (1, 3))
FORTH = (1, 0, 2)
BACK = (0, 1, 2)


def ordered(quarters, order):
    return quarters[:1] + tuple(quarters[1 + number] for number in order)


def deal(quarters, c, refs, above, below):
    tops, bottoms = pieces(above), pieces(below)
    even = c == 0
    for (first, second), out in zip(quarters, refs):
        out[...] = jnp.concatenate(
            [jnp.where(even, part[first], part[second]) for part in (tops, bottoms)], axis=0
        ).astype(bf16)


def gather(quarters, c, refs):
    even = c == 0
    values = [ref[...].astype(f32) for ref in refs]
    chosen = []
    for index in range(4):
        at_even = [first for first, _ in quarters].index(index)
        at_odd = [second for _, second in quarters].index(index)
        chosen.append(jnp.where(even, values[at_even], values[at_odd]))
    return (
        jnp.concatenate([value[:QUAD] for value in chosen], axis=0),
        jnp.concatenate([value[QUAD:] for value in chosen], axis=0),
    )


def one_kernel(
    keep, received, gain, weight_qkv, weight_proj, bias,
    stay, first, second, third, u_out, qkv, probs, mixed,
):
    c = parity()
    k = keep[...].astype(f32)
    r = received[...].astype(f32)
    mine = c == 0
    lead = jnp.where(mine, k, r)
    trail = jnp.where(mine, r, k)
    u = jnp.concatenate([lead[:HALF], trail[:HALF]], axis=0)
    g = jnp.concatenate([lead[HALF:], trail[HALF:]], axis=0)
    u_out[...] = u.astype(bf16)
    normed, _ = norm(u)
    h = (normed * row(gain)).astype(bf16)
    qkv[...] = dot(h, weight_qkv[...]).astype(bf16)
    attend(qkv, bias, probs, mixed)
    middle = u + dot(mixed[...], weight_proj[...])
    deal(ordered(QUARTERS_ONE, FORTH), c, (stay, first, second, third), middle, g)


def two_kernel(
    stay, first, second, third, gain, weight_qkv, weight_proj, weight_qkv_t, weight_proj_t, bias,
    back_stay, back_first, back_second, back_third,
    qkv, probs, mixed, grad_mixed, grad_qkv,
):
    c = parity()
    u, g = gather(ordered(QUARTERS_TWO, FORTH), c, (stay, first, second, third))
    normed, inverse = norm(u)
    h = (normed * row(gain)).astype(bf16)
    qkv[...] = dot(h, weight_qkv[...]).astype(bf16)
    attend(qkv, bias, probs, mixed)
    turned = u + dot(mixed[...], weight_proj[...])
    grad_mixed[...] = dot(g.astype(bf16), weight_proj_t[...]).astype(bf16)
    attend_back(qkv, probs, grad_mixed, grad_qkv)
    dh = dot(grad_qkv[...], weight_qkv_t[...])
    du = g + norm_back(dh, row(gain), normed, inverse)
    deal(ordered(QUARTERS_TWO, BACK), c, (back_stay, back_first, back_second, back_third), du, turned)


def three_kernel(
    stay, first, second, third, u, qkv, probs, gain, weight_qkv_t, weight_proj_t,
    keep, send, grad_mixed, grad_qkv,
):
    c = parity()
    g, turned = gather(ordered(QUARTERS_ONE, BACK), c, (stay, first, second, third))
    normed, inverse = norm(u[...].astype(f32))
    grad_mixed[...] = dot(g.astype(bf16), weight_proj_t[...]).astype(bf16)
    attend_back(qkv, probs, grad_mixed, grad_qkv)
    dh = dot(grad_qkv[...], weight_qkv_t[...])
    du = g + norm_back(dh, row(gain), normed, inverse)
    mine = c == 0
    low = jnp.concatenate([du[:HALF], turned[:HALF]], axis=0)
    high = jnp.concatenate([du[HALF:], turned[HALF:]], axis=0)
    keep[...] = jnp.where(mine, low, high).astype(bf16)
    send[...] = jnp.where(mine, high, low).astype(bf16)


def turn_kernel(weight_qkv, weight_proj, qkv_t, proj_t):
    qkv_t[...] = weight_qkv[...].T
    proj_t[...] = weight_proj[...].T


def shape(*dims, dtype=bf16):
    return jax.ShapeDtypeStruct(dims, dtype)


def call(kernel, outs, scratch, mib, micros, *args, **options):
    return pl.pallas_call(
        kernel,
        out_shape=outs,
        scratch_shapes=scratch,
        compiler_params=pltpu.CompilerParams(vmem_limit_bytes=mib * 1024 * 1024),
        cost_estimate=pl.CostEstimate(
            flops=int(micros * 1e9), bytes_accessed=int(micros * 3e6), transcendentals=0
        ),
        **options,
    )(*args)


def exchange(number, back):
    lats, lons = lax.axis_size("lat"), lax.axis_size("lon")

    def device(a, p, c):
        return a % lats * lons + 2 * p % lons + c

    pairs = []
    for a in range(lats):
        for p in range(lons // 2):
            even, odd = (
                (device(a, p + 1, 0), device(a, p - 1, 1)),
                (device(a - 1, p, 1), device(a, p, 0)),
                (device(a - 1, p - 1, 1), device(a, p + 1, 0)),
            )[number]
            pairs += [(device(a, p, 0), even), (device(a, p, 1), odd)]
    return [(target, source) for source, target in pairs] if back else pairs


def exchanged(values, back):
    return [
        lax.ppermute(value, ("lat", "lon"), exchange(number, back))
        for number, value in zip(BACK if back else FORTH, values)
    ]


def body(
    stream, land, orography, land_vector, orography_table,
    gain_one, qkv_one, proj_one, table_one,
    gain_two, qkv_two, proj_two, table_two, cotangent,
):
    swap = [(i, i ^ 1) for i in range(lax.axis_size("lon"))]
    c = lax.axis_index("lon") % 2

    def flat(array):
        return array.transpose(0, 2, 1, 3).reshape(TOKENS, D)

    def field(array):
        return array.reshape(2, 3, 24, D).transpose(0, 2, 1, 3)

    tokens = shape(TOKENS, D)
    quad = shape(2 * QUAD, D)
    wide = pltpu.VMEM((TOKENS, 3 * D), bf16)
    narrow = pltpu.VMEM((TOKENS, D), bf16)
    keep, send = call(
        pack_kernel, (tokens, tokens),
        [
            narrow, pltpu.VMEM((3, 24), jnp.int32), pltpu.VMEM((3, 24), jnp.int32),
            pltpu.VMEM((D,), f32), pltpu.VMEM((OROG, D), f32), narrow,
            pltpu.SemaphoreType.DMA((6,)),
        ],
        56, 3.0,
        flat(stream), land.T, orography.T, land_vector, orography_table, flat(cotangent),
        in_specs=[pl.BlockSpec(memory_space=pltpu.HBM)] * 6,
    )
    received = lax.ppermute(send, "lon", swap)
    square = shape(HEADS, TOKENS, TOKENS)

    def bias_of(table, masked):
        return call(
            functools.partial(bias_kernel, masked), square,
            [pltpu.VMEM((2, HEADS * 24, 128), f32)] * 2, 8, 1.5,
            lax.dynamic_index_in_dim(table, c, 0, False),
        )

    stay, *leave, u_one, saved_qkv, saved_probs = call(
        one_kernel,
        (quad, quad, quad, quad, tokens, shape(TOKENS, 3 * D), square),
        [narrow], 16, 3.0,
        keep, received, gain_one, qkv_one, proj_one, bias_of(table_one, False),
    )
    table_two, qkv_now, stay = lax.optimization_barrier((table_two, qkv_two, stay))
    turned_shapes = (shape(3 * D, D), shape(D, D))
    qkv_two_t, proj_two_t = call(turn_kernel, turned_shapes, [], 14, 1.5, qkv_now, proj_two)
    arrived = exchanged(leave, False)
    stay, *leave = call(
        two_kernel, (quad, quad, quad, quad),
        [wide, pltpu.VMEM((HEADS, TOKENS, TOKENS), bf16), narrow, narrow, wide], 16, 8.0,
        stay, *arrived, gain_two, qkv_two, proj_two, qkv_two_t, proj_two_t,
        bias_of(table_two, True),
    )
    arrived = exchanged(leave, True)
    qkv_now, stay = lax.optimization_barrier((qkv_one, stay))
    qkv_one_t, proj_one_t = call(turn_kernel, turned_shapes, [], 14, 1.5, qkv_now, proj_one)
    keep, send = call(
        three_kernel, (tokens, tokens), [narrow, wide], 16, 6.0,
        stay, *arrived, u_one, saved_qkv, saved_probs, gain_one, qkv_one_t, proj_one_t,
    )
    received = lax.ppermute(send, "lon", swap)
    output, grad = call(unpack_kernel, (tokens, tokens), [], 8, 1.0, keep, received)
    return field(output), field(grad)


def solution(mesh):
    tokens = P(None, "lat", "lon", None)
    table = P("lat", None, None)
    placed = (
        tokens, P("lat", "lon"), P("lat", "lon"), P(), P(),
        P(), P(), P(), table, P(), P(), P(), table, tokens,
    )
    return jax.shard_map(
        body, mesh=mesh, in_specs=placed, out_specs=(tokens, tokens), check_vma=False
    )
```

```python
import functools

import jax
import jax.numpy as jnp
from jax import lax
from jax.experimental import pallas as pl
from jax.experimental.pallas import tpu as pltpu
from jax.sharding import PartitionSpec as P

D = 768
HEADS = 12
DEPTH = 64
TOKENS = 144
HALF = 72
QUAD = 36
CHUNK = 132
OROG = 8
LAND = 16
EPS = 1e-05

f32 = jnp.float32
bf16 = jnp.bfloat16


def iota(shape, dim):
    return lax.broadcasted_iota(jnp.int32, shape, dim)


def div(a, b):
    return lax.div(a, jnp.int32(b))


def rem(a, b):
    return lax.rem(a, jnp.int32(b))


def dot(a, b):
    return jnp.dot(a, b, preferred_element_type=f32)


def dot_t(a, b):
    return lax.dot_general(a, b, (((1,), (1,)), ((), ())), preferred_element_type=f32)


def t_dot(a, b):
    return lax.dot_general(a, b, (((0,), (0,)), ((), ())), preferred_element_type=f32)


def parity():
    return rem(lax.axis_index("lon").astype(jnp.int32), 2)


def split_token(i):
    level = rem(div(i, 18), 2)
    line = rem(div(i, 36), 2) * 6 + rem(i, 6)
    col = div(i, 72) * 3 + rem(div(i, 6), 3)
    return level, line, col


def natural_place(i, band):
    level = rem(div(i, 18), 2)
    row = band * 12 + div(i, 36) * 6 + rem(i, 6)
    col = rem(div(i, 6), 3)
    return level * 72 + col * 24 + row


def pack_kernel(
    stream_at, land_at, orography_at, vector_at, table_at, cotangent_at, keep, send,
    stream, land, orography, land_vector, orog_table, cotangent, sems,
):
    c = parity()
    copies = [
        pltpu.make_async_copy(source, target, sems.at[index])
        for index, (source, target) in enumerate((
            (stream_at, stream), (cotangent_at, cotangent), (table_at, orog_table),
            (vector_at, land_vector), (land_at, land), (orography_at, orography),
        ))
    ]
    for copy in copies:
        copy.start()
    out = iota((TOKENS, TOKENS), 0)
    own = out < HALF
    place = natural_place(jnp.where(own, out, out - HALF), jnp.where(own, c, 1 - c))
    move = (iota((TOKENS, TOKENS), 1) == place).astype(f32).astype(bf16)
    for copy in copies:
        copy.wait()
    kinds = iota((OROG, 24), 0)
    spare = jnp.zeros((7, D), f32)
    rest = jnp.concatenate([orog_table[...], row(land_vector), spare], axis=0)
    terms = []
    for _ in range(3):
        terms.append(rest.astype(bf16))
        rest = rest - terms[-1].astype(f32)
    terms = jnp.concatenate(terms, axis=0)
    added = []
    for w in range(3):
        onehot = (orography[w : w + 1, :] == kinds).astype(f32)
        share = land[w : w + 1, :].astype(f32) * (1.0 / LAND)
        coded = jnp.concatenate([onehot, share, jnp.zeros((7, 24), f32)], axis=0)
        coded = jnp.concatenate([coded, coded, coded], axis=0).astype(bf16)
        added.append(t_dot(coded, terms))
    added = jnp.concatenate(added + added, axis=0)
    embedded = (stream[...].astype(f32) + added).astype(bf16)
    e = dot(move, embedded)
    g = dot(move, cotangent[...])
    keep[...] = jnp.concatenate([e[:HALF], g[:HALF]], axis=0).astype(bf16)
    send[...] = jnp.concatenate([e[HALF:], g[HALF:]], axis=0).astype(bf16)


def unpack_kernel(keep, received, output, grad):
    c = parity()
    inp = iota((TOKENS, TOKENS), 1)
    own = inp < HALF
    place = natural_place(jnp.where(own, inp, inp - HALF), jnp.where(own, c, 1 - c))
    move = (iota((TOKENS, TOKENS), 0) == place).astype(f32).astype(bf16)
    k = keep[...].astype(f32)
    r = received[...].astype(f32)
    grads = jnp.concatenate([k[:HALF], r[:HALF]], axis=0).astype(bf16)
    turned = jnp.concatenate([k[HALF:], r[HALF:]], axis=0).astype(bf16)
    grad[...] = dot(move, grads).astype(bf16)
    output[...] = dot(move, turned).astype(bf16)


def bias_kernel(masked, table, bias, first, second):
    place = iota((TOKENS, TOKENS), 1)
    level, line, col = split_token(iota((TOKENS, TOKENS), 0))
    spread = (place == col * 24 + level * 12 + line).astype(f32).astype(bf16)
    level, line, col = split_token(iota((256, TOKENS), 1))
    lane = iota((256, TOKENS), 0)
    lane = jnp.where(lane < 128, lane, jnp.where(lane < 252, -1000, lane - 124))
    base = lane - line * 11 + col - 5
    for za in range(2):
        for zc in range(2):
            into = second if zc else first
            for ra in range(12):
                at = ((za * 2 + zc) * 12 + ra) * CHUNK
                for part, skip in enumerate((0, CHUNK - 128)):
                    into[part, pl.ds(za * 12 + ra, HEADS, stride=24), :] = table[
                        :, at + skip : at + skip + 128
                    ].astype(f32)
    low = jnp.concatenate([first[0], first[1]], axis=1).astype(bf16)
    high = jnp.concatenate([second[0], second[1]], axis=1).astype(bf16)
    parts = []
    for i in range(6):
        hit = base == i
        pick_low = (hit & (level == 0)).astype(f32).astype(bf16)
        pick_high = (hit & (level == 1)).astype(f32).astype(bf16)
        parts.append(dot(low, pick_low) + dot(high, pick_high))
    if masked:
        last = (lax.axis_index("lat") == lax.axis_size("lat") - 1) & (parity() == 1)
        half_q = rem(div(iota((TOKENS, TOKENS), 0), QUAD), 2)
        half_k = rem(div(iota((TOKENS, TOKENS), 1), QUAD), 2)
        forbidden = (half_q != half_k) & last
    for n in range(HEADS):
        stacked = jnp.concatenate([part[n * 24 : n * 24 + 24] for part in parts], axis=0)
        one = dot(spread, stacked.astype(bf16))
        if masked:
            one = jnp.where(forbidden, -1e9, one)
        bias[n] = one.astype(bf16).T


def norm(u):
    average = jnp.mean(u, axis=-1, keepdims=True)
    centred = u - average
    inverse = lax.rsqrt(jnp.mean(centred * centred, axis=-1, keepdims=True) + EPS)
    return centred * inverse, inverse


def row(vector):
    return vector[...].reshape(1, D)


def lane_masks(value):
    low = iota((1, 2 * DEPTH), 1) < DEPTH
    return (
        jnp.where(low, value, 0.0).astype(bf16),
        jnp.where(low, 0.0, value).astype(bf16),
    )


def four_masks(value):
    lane = div(iota((1, 4 * DEPTH), 1), DEPTH)
    return [jnp.where(lane == i, value, 0.0).astype(bf16) for i in range(4)]


def attend(qkv, bias, probs, mixed):
    masks = lane_masks(DEPTH ** (-0.5))
    low = iota((TOKENS, 2 * DEPTH), 1) < DEPTH
    for pair in range(HEADS // 2):
        at = pair * 2 * DEPTH
        q2 = qkv[:, at : at + 128]
        k2 = qkv[:, D + at : D + at + 128]
        v2 = qkv[:, 2 * D + at : 2 * D + at + 128]
        both = dot_t(jnp.concatenate([k2 * masks[0], k2 * masks[1]], axis=0), q2)
        turned = []
        for side in range(2):
            n = pair * 2 + side
            scores = both[side * TOKENS : side * TOKENS + TOKENS] + bias[n].astype(f32)
            expo = jnp.exp(scores - jnp.max(scores, axis=0, keepdims=True))
            p = (expo * (1.0 / jnp.sum(expo, axis=0, keepdims=True))).astype(bf16)
            probs[n] = p
            turned.append(p.T)
        both = dot(jnp.concatenate(turned, axis=0), v2)
        mixed[:, at : at + 128] = jnp.where(low, both[:TOKENS], both[TOKENS:]).astype(bf16)


def attend_back(qkv, probs, grad_mixed, grad_qkv):
    masks = four_masks(DEPTH ** (-0.5))
    low = iota((TOKENS, 2 * DEPTH), 1) < DEPTH
    for group in range(HEADS // 4):
        first = group * 4 * DEPTH
        v4 = qkv[:, 2 * D + first : 2 * D + first + 256]
        g4 = grad_mixed[:, first : first + 256]
        all_dp = dot_t(jnp.concatenate([v4 * mask for mask in masks], axis=0), g4)
        for half in range(2):
            at = first + 128 * half
            q2 = qkv[:, at : at + 128]
            k2 = qkv[:, D + at : D + at + 128]
            g2 = grad_mixed[:, at : at + 128]
            ps, ds, ds_t = [], [], []
            for side in range(2):
                n = 2 * half + side
                p = probs[group * 4 + n]
                wide = p.astype(f32)
                dp = all_dp[n * TOKENS : n * TOKENS + TOKENS]
                inner = jnp.sum(wide * dp, axis=0, keepdims=True)
                d = (wide * (dp - inner)).astype(bf16)
                ps.append(p)
                ds.append(d)
                ds_t.append(d.T)
            for block, (lhs, rhs) in enumerate(((ds_t, k2), (ds, q2), (ps, g2))):
                both = dot(jnp.concatenate(lhs, axis=0), rhs)
                grad_qkv[:, block * D + at : block * D + at + 128] = jnp.where(
                    low, both[:TOKENS], both[TOKENS:]
                ).astype(bf16)


def norm_back(dh, gain, normed, inverse):
    dn = dh * gain
    first = jnp.mean(dn, axis=-1, keepdims=True)
    second = jnp.mean(dn * normed, axis=-1, keepdims=True)
    return (dn - first - normed * second) * inverse


def pieces(array):
    return [array[index * QUAD : (index + 1) * QUAD] for index in range(4)]


QUARTERS_ONE = ((1, 3), (3, 1), (2, 0), (0, 2))
QUARTERS_TWO = ((2, 0), (0, 2), (3, 1), (1, 3))
FORTH = (1, 0, 2)
BACK = (2, 0, 1)


def ordered(quarters, order):
    return quarters[:1] + tuple(quarters[1 + number] for number in order)


def deal(quarters, c, refs, above, below):
    tops, bottoms = pieces(above), pieces(below)
    even = c == 0
    for (first, second), out in zip(quarters, refs):
        out[...] = jnp.concatenate(
            [jnp.where(even, part[first], part[second]) for part in (tops, bottoms)], axis=0
        ).astype(bf16)


def gather(quarters, c, refs):
    even = c == 0
    values = [ref[...].astype(f32) for ref in refs]
    chosen = []
    for index in range(4):
        at_even = [first for first, _ in quarters].index(index)
        at_odd = [second for _, second in quarters].index(index)
        chosen.append(jnp.where(even, values[at_even], values[at_odd]))
    return (
        jnp.concatenate([value[:QUAD] for value in chosen], axis=0),
        jnp.concatenate([value[QUAD:] for value in chosen], axis=0),
    )


def one_kernel(
    keep, received, gain, weight_qkv, weight_proj, bias,
    stay, first, second, third, u_out, qkv, probs, mixed,
):
    c = parity()
    k = keep[...].astype(f32)
    r = received[...].astype(f32)
    mine = c == 0
    lead = jnp.where(mine, k, r)
    trail = jnp.where(mine, r, k)
    u = jnp.concatenate([lead[:HALF], trail[:HALF]], axis=0)
    g = jnp.concatenate([lead[HALF:], trail[HALF:]], axis=0)
    u_out[...] = u.astype(bf16)
    normed, _ = norm(u)
    h = (normed * row(gain)).astype(bf16)
    qkv[...] = dot(h, weight_qkv[...]).astype(bf16)
    attend(qkv, bias, probs, mixed)
    middle = u + dot(mixed[...], weight_proj[...])
    deal(ordered(QUARTERS_ONE, FORTH), c, (stay, first, second, third), middle, g)


def two_kernel(
    stay, first, second, third, gain, weight_qkv, weight_proj, weight_qkv_t, weight_proj_t, bias,
    back_stay, back_first, back_second, back_third,
    qkv, probs, mixed, grad_mixed, grad_qkv,
):
    c = parity()
    u, g = gather(ordered(QUARTERS_TWO, FORTH), c, (stay, first, second, third))
    normed, inverse = norm(u)
    h = (normed * row(gain)).astype(bf16)
    qkv[...] = dot(h, weight_qkv[...]).astype(bf16)
    attend(qkv, bias, probs, mixed)
    turned = u + dot(mixed[...], weight_proj[...])
    grad_mixed[...] = dot(g.astype(bf16), weight_proj_t[...]).astype(bf16)
    attend_back(qkv, probs, grad_mixed, grad_qkv)
    dh = dot(grad_qkv[...], weight_qkv_t[...])
    du = g + norm_back(dh, row(gain), normed, inverse)
    deal(ordered(QUARTERS_TWO, BACK), c, (back_stay, back_first, back_second, back_third), du, turned)


def three_kernel(
    stay, first, second, third, u, qkv, probs, gain, weight_qkv_t, weight_proj_t,
    keep, send, grad_mixed, grad_qkv,
):
    c = parity()
    g, turned = gather(ordered(QUARTERS_ONE, BACK), c, (stay, first, second, third))
    normed, inverse = norm(u[...].astype(f32))
    grad_mixed[...] = dot(g.astype(bf16), weight_proj_t[...]).astype(bf16)
    attend_back(qkv, probs, grad_mixed, grad_qkv)
    dh = dot(grad_qkv[...], weight_qkv_t[...])
    du = g + norm_back(dh, row(gain), normed, inverse)
    mine = c == 0
    low = jnp.concatenate([du[:HALF], turned[:HALF]], axis=0)
    high = jnp.concatenate([du[HALF:], turned[HALF:]], axis=0)
    keep[...] = jnp.where(mine, low, high).astype(bf16)
    send[...] = jnp.where(mine, high, low).astype(bf16)


def turn_kernel(weight_qkv, weight_proj, qkv_t, proj_t):
    qkv_t[...] = weight_qkv[...].T
    proj_t[...] = weight_proj[...].T


def shape(*dims, dtype=bf16):
    return jax.ShapeDtypeStruct(dims, dtype)


def call(kernel, outs, scratch, mib, micros, *args, **options):
    return pl.pallas_call(
        kernel,
        out_shape=outs,
        scratch_shapes=scratch,
        compiler_params=pltpu.CompilerParams(vmem_limit_bytes=mib * 1024 * 1024),
        cost_estimate=pl.CostEstimate(
            flops=int(micros * 1e9), bytes_accessed=int(micros * 3e6), transcendentals=0
        ),
        **options,
    )(*args)


def exchange(number, back):
    lats, lons = lax.axis_size("lat"), lax.axis_size("lon")

    def device(a, p, c):
        return a % lats * lons + 2 * p % lons + c

    pairs = []
    for a in range(lats):
        for p in range(lons // 2):
            even, odd = (
                (device(a, p + 1, 0), device(a, p - 1, 1)),
                (device(a - 1, p, 1), device(a, p, 0)),
                (device(a - 1, p - 1, 1), device(a, p + 1, 0)),
            )[number]
            pairs += [(device(a, p, 0), even), (device(a, p, 1), odd)]
    return [(target, source) for source, target in pairs] if back else pairs


def exchanged(values, back):
    return [
        lax.ppermute(value, ("lat", "lon"), exchange(number, back))
        for number, value in zip(BACK if back else FORTH, values)
    ]


def body(
    stream, land, orography, land_vector, orography_table,
    gain_one, qkv_one, proj_one, table_one,
    gain_two, qkv_two, proj_two, table_two, cotangent,
):
    swap = [(i, i ^ 1) for i in range(lax.axis_size("lon"))]
    c = lax.axis_index("lon") % 2

    def flat(array):
        return array.transpose(0, 2, 1, 3).reshape(TOKENS, D)

    def field(array):
        return array.reshape(2, 3, 24, D).transpose(0, 2, 1, 3)

    tokens = shape(TOKENS, D)
    quad = shape(2 * QUAD, D)
    wide = pltpu.VMEM((TOKENS, 3 * D), bf16)
    narrow = pltpu.VMEM((TOKENS, D), bf16)
    keep, send = call(
        pack_kernel, (tokens, tokens),
        [
            narrow, pltpu.VMEM((3, 24), jnp.int32), pltpu.VMEM((3, 24), jnp.int32),
            pltpu.VMEM((D,), f32), pltpu.VMEM((OROG, D), f32), narrow,
            pltpu.SemaphoreType.DMA((6,)),
        ],
        56, 3.0,
        flat(stream), land.T, orography.T, land_vector, orography_table, flat(cotangent),
        in_specs=[pl.BlockSpec(memory_space=pltpu.HBM)] * 6,
    )
    received = lax.ppermute(send, "lon", swap)
    square = shape(HEADS, TOKENS, TOKENS)

    def bias_of(table, masked):
        return call(
            functools.partial(bias_kernel, masked), square,
            [pltpu.VMEM((2, HEADS * 24, 128), f32)] * 2, 8, 1.5,
            lax.dynamic_index_in_dim(table, c, 0, False),
        )

    stay, *leave, u_one, saved_qkv, saved_probs = call(
        one_kernel,
        (quad, quad, quad, quad, tokens, shape(TOKENS, 3 * D), square),
        [narrow], 16, 3.0,
        keep, received, gain_one, qkv_one, proj_one, bias_of(table_one, False),
    )
    table_two, qkv_now, stay = lax.optimization_barrier((table_two, qkv_two, stay))
    turned_shapes = (shape(3 * D, D), shape(D, D))
    qkv_two_t, proj_two_t = call(turn_kernel, turned_shapes, [], 14, 1.5, qkv_now, proj_two)
    arrived = exchanged(leave, False)
    stay, *leave = call(
        two_kernel, (quad, quad, quad, quad),
        [wide, pltpu.VMEM((HEADS, TOKENS, TOKENS), bf16), narrow, narrow, wide], 16, 8.0,
        stay, *arrived, gain_two, qkv_two, proj_two, qkv_two_t, proj_two_t,
        bias_of(table_two, True),
    )
    arrived = exchanged(leave, True)
    qkv_now, stay = lax.optimization_barrier((qkv_one, stay))
    qkv_one_t, proj_one_t = call(turn_kernel, turned_shapes, [], 14, 1.5, qkv_now, proj_one)
    keep, send = call(
        three_kernel, (tokens, tokens), [narrow, wide], 16, 6.0,
        stay, *arrived, u_one, saved_qkv, saved_probs, gain_one, qkv_one_t, proj_one_t,
    )
    received = lax.ppermute(send, "lon", swap)
    output, grad = call(unpack_kernel, (tokens, tokens), [], 8, 1.0, keep, received)
    return field(output), field(grad)


def solution(mesh):
    tokens = P(None, "lat", "lon", None)
    table = P("lat", None, None)
    placed = (
        tokens, P("lat", "lon"), P("lat", "lon"), P(), P(),
        P(), P(), P(), table, P(), P(), P(), table, tokens,
    )
    return jax.shard_map(
        body, mesh=mesh, in_specs=placed, out_specs=(tokens, tokens), check_vma=False
    )
```

```python
import functools

import jax
import jax.numpy as jnp
from jax import lax
from jax.experimental import pallas as pl
from jax.experimental.pallas import tpu as pltpu
from jax.sharding import PartitionSpec as P

D = 768
HEADS = 12
DEPTH = 64
TOKENS = 144
HALF = 72
QUAD = 36
CHUNK = 132
OROG = 8
LAND = 16
EPS = 1e-05

f32 = jnp.float32
bf16 = jnp.bfloat16


def iota(shape, dim):
    return lax.broadcasted_iota(jnp.int32, shape, dim)


def div(a, b):
    return lax.div(a, jnp.int32(b))


def rem(a, b):
    return lax.rem(a, jnp.int32(b))


def dot(a, b):
    return jnp.dot(a, b, preferred_element_type=f32)


def dot_t(a, b):
    return lax.dot_general(a, b, (((1,), (1,)), ((), ())), preferred_element_type=f32)


def t_dot(a, b):
    return lax.dot_general(a, b, (((0,), (0,)), ((), ())), preferred_element_type=f32)


def parity():
    return rem(lax.axis_index("lon").astype(jnp.int32), 2)


def split_token(i):
    level = rem(div(i, 18), 2)
    line = rem(div(i, 36), 2) * 6 + rem(i, 6)
    col = div(i, 72) * 3 + rem(div(i, 6), 3)
    return level, line, col


def natural_place(i, band):
    level = rem(div(i, 18), 2)
    row = band * 12 + div(i, 36) * 6 + rem(i, 6)
    col = rem(div(i, 6), 3)
    return level * 72 + col * 24 + row


def pack_kernel(
    stream_at, land_at, orography_at, vector_at, table_at, cotangent_at, keep, send,
    stream, land, orography, land_vector, orog_table, cotangent, sems,
):
    c = parity()
    copies = [
        pltpu.make_async_copy(source, target, sems.at[index])
        for index, (source, target) in enumerate((
            (stream_at, stream), (cotangent_at, cotangent), (table_at, orog_table),
            (vector_at, land_vector), (land_at, land), (orography_at, orography),
        ))
    ]
    for copy in copies:
        copy.start()
    out = iota((TOKENS, TOKENS), 0)
    own = out < HALF
    place = natural_place(jnp.where(own, out, out - HALF), jnp.where(own, c, 1 - c))
    move = (iota((TOKENS, TOKENS), 1) == place).astype(f32).astype(bf16)
    for copy in copies:
        copy.wait()
    kinds = iota((OROG, 24), 0)
    spare = jnp.zeros((7, D), f32)
    rest = jnp.concatenate([orog_table[...], row(land_vector), spare], axis=0)
    terms = []
    for _ in range(3):
        terms.append(rest.astype(bf16))
        rest = rest - terms[-1].astype(f32)
    terms = jnp.concatenate(terms, axis=0)
    added = []
    for w in range(3):
        onehot = (orography[w : w + 1, :] == kinds).astype(f32)
        share = land[w : w + 1, :].astype(f32) * (1.0 / LAND)
        coded = jnp.concatenate([onehot, share, jnp.zeros((7, 24), f32)], axis=0)
        coded = jnp.concatenate([coded, coded, coded], axis=0).astype(bf16)
        added.append(t_dot(coded, terms))
    added = jnp.concatenate(added + added, axis=0)
    embedded = (stream[...].astype(f32) + added).astype(bf16)
    e = dot(move, embedded)
    g = dot(move, cotangent[...])
    keep[...] = jnp.concatenate([e[:HALF], g[:HALF]], axis=0).astype(bf16)
    send[...] = jnp.concatenate([e[HALF:], g[HALF:]], axis=0).astype(bf16)


def unpack_kernel(keep, received, output, grad):
    c = parity()
    inp = iota((TOKENS, TOKENS), 1)
    own = inp < HALF
    place = natural_place(jnp.where(own, inp, inp - HALF), jnp.where(own, c, 1 - c))
    move = (iota((TOKENS, TOKENS), 0) == place).astype(f32).astype(bf16)
    k = keep[...].astype(f32)
    r = received[...].astype(f32)
    grads = jnp.concatenate([k[:HALF], r[:HALF]], axis=0).astype(bf16)
    turned = jnp.concatenate([k[HALF:], r[HALF:]], axis=0).astype(bf16)
    grad[...] = dot(move, grads).astype(bf16)
    output[...] = dot(move, turned).astype(bf16)


def bias_kernel(masked, table, bias, first, second):
    place = iota((TOKENS, TOKENS), 1)
    level, line, col = split_token(iota((TOKENS, TOKENS), 0))
    spread = (place == col * 24 + level * 12 + line).astype(f32).astype(bf16)
    level, line, col = split_token(iota((256, TOKENS), 1))
    lane = iota((256, TOKENS), 0)
    lane = jnp.where(lane < 128, lane, jnp.where(lane < 252, -1000, lane - 124))
    base = lane - line * 11 + col - 5
    for za in range(2):
        for zc in range(2):
            into = second if zc else first
            for ra in range(12):
                at = ((za * 2 + zc) * 12 + ra) * CHUNK
                for part, skip in enumerate((0, CHUNK - 128)):
                    into[part, pl.ds(za * 12 + ra, HEADS, stride=24), :] = table[
                        :, at + skip : at + skip + 128
                    ].astype(f32)
    low = jnp.concatenate([first[0], first[1]], axis=1).astype(bf16)
    high = jnp.concatenate([second[0], second[1]], axis=1).astype(bf16)
    parts = []
    for i in range(6):
        hit = base == i
        pick_low = (hit & (level == 0)).astype(f32).astype(bf16)
        pick_high = (hit & (level == 1)).astype(f32).astype(bf16)
        parts.append(dot(low, pick_low) + dot(high, pick_high))
    if masked:
        last = (lax.axis_index("lat") == lax.axis_size("lat") - 1) & (parity() == 1)
        half_q = rem(div(iota((TOKENS, TOKENS), 0), QUAD), 2)
        half_k = rem(div(iota((TOKENS, TOKENS), 1), QUAD), 2)
        forbidden = (half_q != half_k) & last
    for n in range(HEADS):
        stacked = jnp.concatenate([part[n * 24 : n * 24 + 24] for part in parts], axis=0)
        one = dot(spread, stacked.astype(bf16))
        if masked:
            one = jnp.where(forbidden, -1e9, one)
        bias[n] = one.astype(bf16).T


def norm(u):
    average = jnp.mean(u, axis=-1, keepdims=True)
    centred = u - average
    inverse = lax.rsqrt(jnp.mean(centred * centred, axis=-1, keepdims=True) + EPS)
    return centred * inverse, inverse


def row(vector):
    return vector[...].reshape(1, D)


def lane_masks(value):
    low = iota((1, 2 * DEPTH), 1) < DEPTH
    return (
        jnp.where(low, value, 0.0).astype(bf16),
        jnp.where(low, 0.0, value).astype(bf16),
    )


def four_masks(value):
    lane = div(iota((1, 4 * DEPTH), 1), DEPTH)
    return [jnp.where(lane == i, value, 0.0).astype(bf16) for i in range(4)]


def attend(qkv, bias, probs, mixed):
    masks = lane_masks(DEPTH ** (-0.5))
    low = iota((TOKENS, 2 * DEPTH), 1) < DEPTH
    for pair in range(HEADS // 2):
        at = pair * 2 * DEPTH
        q2 = qkv[:, at : at + 128]
        k2 = qkv[:, D + at : D + at + 128]
        v2 = qkv[:, 2 * D + at : 2 * D + at + 128]
        both = dot_t(jnp.concatenate([k2 * masks[0], k2 * masks[1]], axis=0), q2)
        turned = []
        for side in range(2):
            n = pair * 2 + side
            scores = both[side * TOKENS : side * TOKENS + TOKENS] + bias[n].astype(f32)
            expo = jnp.exp(scores - jnp.max(scores, axis=0, keepdims=True))
            p = (expo * (1.0 / jnp.sum(expo, axis=0, keepdims=True))).astype(bf16)
            probs[n] = p
            turned.append(p.T)
        both = dot(jnp.concatenate(turned, axis=0), v2)
        mixed[:, at : at + 128] = jnp.where(low, both[:TOKENS], both[TOKENS:]).astype(bf16)


def attend_back(qkv, probs, grad_mixed, grad_qkv):
    masks = four_masks(DEPTH ** (-0.5))
    ones = four_masks(1.0)
    low = iota((TOKENS, 2 * DEPTH), 1) < DEPTH
    for group in range(HEADS // 4):
        first = group * 4 * DEPTH
        v4 = qkv[:, 2 * D + first : 2 * D + first + 256]
        g4 = grad_mixed[:, first : first + 256]
        all_dp = dot_t(jnp.concatenate([v4 * mask for mask in masks], axis=0), g4)
        k4 = qkv[:, D + first : D + first + 256]
        slopes = []
        for half in range(2):
            at = first + 128 * half
            q2 = qkv[:, at : at + 128]
            g2 = grad_mixed[:, at : at + 128]
            ps, ds = [], []
            for side in range(2):
                n = 2 * half + side
                p = probs[group * 4 + n]
                wide = p.astype(f32)
                dp = all_dp[n * TOKENS : n * TOKENS + TOKENS]
                inner = jnp.sum(wide * dp, axis=0, keepdims=True)
                d = (wide * (dp - inner)).astype(bf16)
                ps.append(p)
                ds.append(d)
            for block, (lhs, rhs) in enumerate(((ds, q2), (ps, g2))):
                both = dot(jnp.concatenate(lhs, axis=0), rhs)
                grad_qkv[:, (block + 1) * D + at : (block + 1) * D + at + 128] = jnp.where(
                    low, both[:TOKENS], both[TOKENS:]
                ).astype(bf16)
            slopes += ds
        keys = jnp.concatenate([k4 * mask for mask in ones], axis=0)
        grad_qkv[:, first : first + 256] = dot(
            jnp.concatenate(slopes, axis=0).T, keys
        ).astype(bf16)


def norm_back(dh, gain, normed, inverse):
    dn = dh * gain
    first = jnp.mean(dn, axis=-1, keepdims=True)
    second = jnp.mean(dn * normed, axis=-1, keepdims=True)
    return (dn - first - normed * second) * inverse


def pieces(array):
    return [array[index * QUAD : (index + 1) * QUAD] for index in range(4)]


QUARTERS_ONE = ((1, 3), (3, 1), (2, 0), (0, 2))
QUARTERS_TWO = ((2, 0), (0, 2), (3, 1), (1, 3))
FORTH = (1, 0, 2)
BACK = (2, 0, 1)


def ordered(quarters, order):
    return quarters[:1] + tuple(quarters[1 + number] for number in order)


def deal(quarters, c, refs, above, below):
    tops, bottoms = pieces(above), pieces(below)
    even = c == 0
    for (first, second), out in zip(quarters, refs):
        out[...] = jnp.concatenate(
            [jnp.where(even, part[first], part[second]) for part in (tops, bottoms)], axis=0
        ).astype(bf16)


def gather(quarters, c, refs):
    even = c == 0
    values = [ref[...].astype(f32) for ref in refs]
    chosen = []
    for index in range(4):
        at_even = [first for first, _ in quarters].index(index)
        at_odd = [second for _, second in quarters].index(index)
        chosen.append(jnp.where(even, values[at_even], values[at_odd]))
    return (
        jnp.concatenate([value[:QUAD] for value in chosen], axis=0),
        jnp.concatenate([value[QUAD:] for value in chosen], axis=0),
    )


def one_kernel(
    keep, received, gain, weight_qkv, weight_proj, bias,
    stay, first, second, third, u_out, qkv, probs, mixed,
):
    c = parity()
    k = keep[...].astype(f32)
    r = received[...].astype(f32)
    mine = c == 0
    lead = jnp.where(mine, k, r)
    trail = jnp.where(mine, r, k)
    u = jnp.concatenate([lead[:HALF], trail[:HALF]], axis=0)
    g = jnp.concatenate([lead[HALF:], trail[HALF:]], axis=0)
    u_out[...] = u.astype(bf16)
    normed, _ = norm(u)
    h = (normed * row(gain)).astype(bf16)
    qkv[...] = dot(h, weight_qkv[...]).astype(bf16)
    attend(qkv, bias, probs, mixed)
    middle = u + dot(mixed[...], weight_proj[...])
    deal(ordered(QUARTERS_ONE, FORTH), c, (stay, first, second, third), middle, g)


def two_kernel(
    stay, first, second, third, gain, weight_qkv, weight_proj, weight_qkv_t, weight_proj_t, bias,
    back_stay, back_first, back_second, back_third,
    qkv, probs, mixed, grad_mixed, grad_qkv,
):
    c = parity()
    u, g = gather(ordered(QUARTERS_TWO, FORTH), c, (stay, first, second, third))
    normed, inverse = norm(u)
    h = (normed * row(gain)).astype(bf16)
    qkv[...] = dot(h, weight_qkv[...]).astype(bf16)
    attend(qkv, bias, probs, mixed)
    turned = u + dot(mixed[...], weight_proj[...])
    grad_mixed[...] = dot(g.astype(bf16), weight_proj_t[...]).astype(bf16)
    attend_back(qkv, probs, grad_mixed, grad_qkv)
    dh = dot(grad_qkv[...], weight_qkv_t[...])
    du = g + norm_back(dh, row(gain), normed, inverse)
    deal(ordered(QUARTERS_TWO, BACK), c, (back_stay, back_first, back_second, back_third), du, turned)


def three_kernel(
    stay, first, second, third, u, qkv, probs, gain, weight_qkv_t, weight_proj_t,
    keep, send, grad_mixed, grad_qkv,
):
    c = parity()
    g, turned = gather(ordered(QUARTERS_ONE, BACK), c, (stay, first, second, third))
    normed, inverse = norm(u[...].astype(f32))
    grad_mixed[...] = dot(g.astype(bf16), weight_proj_t[...]).astype(bf16)
    attend_back(qkv, probs, grad_mixed, grad_qkv)
    dh = dot(grad_qkv[...], weight_qkv_t[...])
    du = g + norm_back(dh, row(gain), normed, inverse)
    mine = c == 0
    low = jnp.concatenate([du[:HALF], turned[:HALF]], axis=0)
    high = jnp.concatenate([du[HALF:], turned[HALF:]], axis=0)
    keep[...] = jnp.where(mine, low, high).astype(bf16)
    send[...] = jnp.where(mine, high, low).astype(bf16)


def turn_kernel(weight_qkv, weight_proj, qkv_t, proj_t):
    qkv_t[...] = weight_qkv[...].T
    proj_t[...] = weight_proj[...].T


def shape(*dims, dtype=bf16):
    return jax.ShapeDtypeStruct(dims, dtype)


def call(kernel, outs, scratch, mib, micros, *args, **options):
    return pl.pallas_call(
        kernel,
        out_shape=outs,
        scratch_shapes=scratch,
        compiler_params=pltpu.CompilerParams(vmem_limit_bytes=mib * 1024 * 1024),
        cost_estimate=pl.CostEstimate(
            flops=int(micros * 1e9), bytes_accessed=int(micros * 3e6), transcendentals=0
        ),
        **options,
    )(*args)


def exchange(number, back):
    lats, lons = lax.axis_size("lat"), lax.axis_size("lon")

    def device(a, p, c):
        return a % lats * lons + 2 * p % lons + c

    pairs = []
    for a in range(lats):
        for p in range(lons // 2):
            even, odd = (
                (device(a, p + 1, 0), device(a, p - 1, 1)),
                (device(a - 1, p, 1), device(a, p, 0)),
                (device(a - 1, p - 1, 1), device(a, p + 1, 0)),
            )[number]
            pairs += [(device(a, p, 0), even), (device(a, p, 1), odd)]
    return [(target, source) for source, target in pairs] if back else pairs


def exchanged(values, back):
    return [
        lax.ppermute(value, ("lat", "lon"), exchange(number, back))
        for number, value in zip(BACK if back else FORTH, values)
    ]


def body(
    stream, land, orography, land_vector, orography_table,
    gain_one, qkv_one, proj_one, table_one,
    gain_two, qkv_two, proj_two, table_two, cotangent,
):
    swap = [(i, i ^ 1) for i in range(lax.axis_size("lon"))]
    c = lax.axis_index("lon") % 2

    def flat(array):
        return array.transpose(0, 2, 1, 3).reshape(TOKENS, D)

    def field(array):
        return array.reshape(2, 3, 24, D).transpose(0, 2, 1, 3)

    tokens = shape(TOKENS, D)
    quad = shape(2 * QUAD, D)
    wide = pltpu.VMEM((TOKENS, 3 * D), bf16)
    narrow = pltpu.VMEM((TOKENS, D), bf16)
    keep, send = call(
        pack_kernel, (tokens, tokens),
        [
            narrow, pltpu.VMEM((3, 24), jnp.int32), pltpu.VMEM((3, 24), jnp.int32),
            pltpu.VMEM((D,), f32), pltpu.VMEM((OROG, D), f32), narrow,
            pltpu.SemaphoreType.DMA((6,)),
        ],
        56, 3.0,
        flat(stream), land.T, orography.T, land_vector, orography_table, flat(cotangent),
        in_specs=[pl.BlockSpec(memory_space=pltpu.HBM)] * 6,
    )
    received = lax.ppermute(send, "lon", swap)
    square = shape(HEADS, TOKENS, TOKENS)

    def bias_of(table, masked):
        return call(
            functools.partial(bias_kernel, masked), square,
            [pltpu.VMEM((2, HEADS * 24, 128), f32)] * 2, 8, 1.5,
            lax.dynamic_index_in_dim(table, c, 0, False),
        )

    stay, *leave, u_one, saved_qkv, saved_probs = call(
        one_kernel,
        (quad, quad, quad, quad, tokens, shape(TOKENS, 3 * D), square),
        [narrow], 16, 3.0,
        keep, received, gain_one, qkv_one, proj_one, bias_of(table_one, False),
    )
    table_two, qkv_now, stay = lax.optimization_barrier((table_two, qkv_two, stay))
    turned_shapes = (shape(3 * D, D), shape(D, D))
    qkv_two_t, proj_two_t = call(turn_kernel, turned_shapes, [], 14, 1.5, qkv_now, proj_two)
    arrived = exchanged(leave, False)
    stay, *leave = call(
        two_kernel, (quad, quad, quad, quad),
        [wide, pltpu.VMEM((HEADS, TOKENS, TOKENS), bf16), narrow, narrow, wide], 16, 8.0,
        stay, *arrived, gain_two, qkv_two, proj_two, qkv_two_t, proj_two_t,
        bias_of(table_two, True),
    )
    arrived = exchanged(leave, True)
    qkv_now, stay = lax.optimization_barrier((qkv_one, stay))
    qkv_one_t, proj_one_t = call(turn_kernel, turned_shapes, [], 14, 1.5, qkv_now, proj_one)
    keep, send = call(
        three_kernel, (tokens, tokens), [narrow, wide], 16, 6.0,
        stay, *arrived, u_one, saved_qkv, saved_probs, gain_one, qkv_one_t, proj_one_t,
    )
    received = lax.ppermute(send, "lon", swap)
    output, grad = call(unpack_kernel, (tokens, tokens), [], 8, 1.0, keep, received)
    return field(output), field(grad)


def solution(mesh):
    tokens = P(None, "lat", "lon", None)
    table = P("lat", None, None)
    placed = (
        tokens, P("lat", "lon"), P("lat", "lon"), P(), P(),
        P(), P(), P(), table, P(), P(), P(), table, tokens,
    )
    return jax.shard_map(
        body, mesh=mesh, in_specs=placed, out_specs=(tokens, tokens), check_vma=False
    )
```

```python
import functools

import jax
import jax.numpy as jnp
from jax import lax
from jax.experimental import pallas as pl
from jax.experimental.pallas import tpu as pltpu
from jax.sharding import PartitionSpec as P

D = 768
HEADS = 12
DEPTH = 64
TOKENS = 144
HALF = 72
QUAD = 36
CHUNK = 132
OROG = 8
LAND = 16
EPS = 1e-05

f32 = jnp.float32
bf16 = jnp.bfloat16


def iota(shape, dim):
    return lax.broadcasted_iota(jnp.int32, shape, dim)


def div(a, b):
    return lax.div(a, jnp.int32(b))


def rem(a, b):
    return lax.rem(a, jnp.int32(b))


def dot(a, b):
    return jnp.dot(a, b, preferred_element_type=f32)


def dot_t(a, b):
    return lax.dot_general(a, b, (((1,), (1,)), ((), ())), preferred_element_type=f32)


def t_dot(a, b):
    return lax.dot_general(a, b, (((0,), (0,)), ((), ())), preferred_element_type=f32)


def parity():
    return rem(lax.axis_index("lon").astype(jnp.int32), 2)


def split_token(i):
    level = rem(div(i, 18), 2)
    line = rem(div(i, 36), 2) * 6 + rem(i, 6)
    col = div(i, 72) * 3 + rem(div(i, 6), 3)
    return level, line, col


def natural_place(i, band):
    level = rem(div(i, 18), 2)
    row = band * 12 + div(i, 36) * 6 + rem(i, 6)
    col = rem(div(i, 6), 3)
    return level * 72 + col * 24 + row


def pack_kernel(
    stream_at, land_at, orography_at, vector_at, table_at, cotangent_at, keep, send,
    stream, land, orography, land_vector, orog_table, cotangent, sems,
):
    c = parity()
    copies = [
        pltpu.make_async_copy(source, target, sems.at[index])
        for index, (source, target) in enumerate((
            (stream_at, stream), (cotangent_at, cotangent), (table_at, orog_table),
            (vector_at, land_vector), (land_at, land), (orography_at, orography),
        ))
    ]
    for copy in copies:
        copy.start()
    out = iota((TOKENS, TOKENS), 0)
    own = out < HALF
    place = natural_place(jnp.where(own, out, out - HALF), jnp.where(own, c, 1 - c))
    move = (iota((TOKENS, TOKENS), 1) == place).astype(f32).astype(bf16)
    for copy in copies:
        copy.wait()
    kinds = iota((OROG, 24), 0)
    spare = jnp.zeros((7, D), f32)
    rest = jnp.concatenate([orog_table[...], row(land_vector), spare], axis=0)
    terms = []
    for _ in range(3):
        terms.append(rest.astype(bf16))
        rest = rest - terms[-1].astype(f32)
    terms = jnp.concatenate(terms, axis=0)
    added = []
    for w in range(3):
        onehot = (orography[w : w + 1, :] == kinds).astype(f32)
        share = land[w : w + 1, :].astype(f32) * (1.0 / LAND)
        coded = jnp.concatenate([onehot, share, jnp.zeros((7, 24), f32)], axis=0)
        coded = jnp.concatenate([coded, coded, coded], axis=0).astype(bf16)
        added.append(t_dot(coded, terms))
    added = jnp.concatenate(added + added, axis=0)
    embedded = (stream[...].astype(f32) + added).astype(bf16)
    e = dot(move, embedded)
    g = dot(move, cotangent[...])
    keep[...] = jnp.concatenate([e[:HALF], g[:HALF]], axis=0).astype(bf16)
    send[...] = jnp.concatenate([e[HALF:], g[HALF:]], axis=0).astype(bf16)


def unpack_kernel(keep, received, output, grad):
    c = parity()
    inp = iota((TOKENS, TOKENS), 1)
    own = inp < HALF
    place = natural_place(jnp.where(own, inp, inp - HALF), jnp.where(own, c, 1 - c))
    move = (iota((TOKENS, TOKENS), 0) == place).astype(f32).astype(bf16)
    k = keep[...].astype(f32)
    r = received[...].astype(f32)
    grads = jnp.concatenate([k[:HALF], r[:HALF]], axis=0).astype(bf16)
    turned = jnp.concatenate([k[HALF:], r[HALF:]], axis=0).astype(bf16)
    grad[...] = dot(move, grads).astype(bf16)
    output[...] = dot(move, turned).astype(bf16)


def bias_kernel(masked, table, bias, first, second):
    place = iota((TOKENS, TOKENS), 1)
    level, line, col = split_token(iota((TOKENS, TOKENS), 0))
    spread = (place == col * 24 + level * 12 + line).astype(f32).astype(bf16)
    level, line, col = split_token(iota((256, TOKENS), 1))
    lane = iota((256, TOKENS), 0)
    lane = jnp.where(lane < 128, lane, jnp.where(lane < 252, -1000, lane - 124))
    base = lane - line * 11 + col - 5
    for za in range(2):
        for zc in range(2):
            into = second if zc else first
            for ra in range(12):
                at = ((za * 2 + zc) * 12 + ra) * CHUNK
                for part, skip in enumerate((0, CHUNK - 128)):
                    into[part, pl.ds(za * 12 + ra, HEADS, stride=24), :] = table[
                        :, at + skip : at + skip + 128
                    ].astype(f32)
    low = jnp.concatenate([first[0], first[1]], axis=1).astype(bf16)
    high = jnp.concatenate([second[0], second[1]], axis=1).astype(bf16)
    parts = []
    for i in range(6):
        hit = base == i
        pick_low = (hit & (level == 0)).astype(f32).astype(bf16)
        pick_high = (hit & (level == 1)).astype(f32).astype(bf16)
        parts.append(dot(low, pick_low) + dot(high, pick_high))
    if masked:
        last = (lax.axis_index("lat") == lax.axis_size("lat") - 1) & (parity() == 1)
        half_q = rem(div(iota((TOKENS, TOKENS), 0), QUAD), 2)
        half_k = rem(div(iota((TOKENS, TOKENS), 1), QUAD), 2)
        forbidden = (half_q != half_k) & last
    for n in range(HEADS):
        stacked = jnp.concatenate([part[n * 24 : n * 24 + 24] for part in parts], axis=0)
        one = dot(spread, stacked.astype(bf16))
        if masked:
            one = jnp.where(forbidden, -1e9, one)
        bias[n] = one.astype(bf16).T


def norm(u):
    average = jnp.mean(u, axis=-1, keepdims=True)
    centred = u - average
    inverse = lax.rsqrt(jnp.mean(centred * centred, axis=-1, keepdims=True) + EPS)
    return centred * inverse, inverse


def row(vector):
    return vector[...].reshape(1, D)


def lane_masks(value):
    low = iota((1, 2 * DEPTH), 1) < DEPTH
    return (
        jnp.where(low, value, 0.0).astype(bf16),
        jnp.where(low, 0.0, value).astype(bf16),
    )


def four_masks(value):
    lane = div(iota((1, 4 * DEPTH), 1), DEPTH)
    return [jnp.where(lane == i, value, 0.0).astype(bf16) for i in range(4)]


def attend(qkv, bias, probs, mixed):
    masks = lane_masks(DEPTH ** (-0.5))
    low = iota((TOKENS, 2 * DEPTH), 1) < DEPTH
    for pair in range(HEADS // 2):
        at = pair * 2 * DEPTH
        q2 = qkv[:, at : at + 128]
        k2 = qkv[:, D + at : D + at + 128]
        v2 = qkv[:, 2 * D + at : 2 * D + at + 128]
        both = dot_t(jnp.concatenate([k2 * masks[0], k2 * masks[1]], axis=0), q2)
        turned = []
        for side in range(2):
            n = pair * 2 + side
            scores = both[side * TOKENS : side * TOKENS + TOKENS] + bias[n].astype(f32)
            expo = jnp.exp(scores - jnp.max(scores, axis=0, keepdims=True))
            p = (expo * (1.0 / jnp.sum(expo, axis=0, keepdims=True))).astype(bf16)
            probs[n] = p
            turned.append(p.T)
        both = dot(jnp.concatenate(turned, axis=0), v2)
        mixed[:, at : at + 128] = jnp.where(low, both[:TOKENS], both[TOKENS:]).astype(bf16)


def attend_back(qkv, probs, grad_mixed, grad_qkv):
    masks = four_masks(DEPTH ** (-0.5))
    low = iota((TOKENS, 2 * DEPTH), 1) < DEPTH
    for group in range(HEADS // 4):
        first = group * 4 * DEPTH
        v4 = qkv[:, 2 * D + first : 2 * D + first + 256]
        g4 = grad_mixed[:, first : first + 256]
        all_dp = dot_t(jnp.concatenate([v4 * mask for mask in masks], axis=0), g4)
        for half in range(2):
            at = first + 128 * half
            q2 = qkv[:, at : at + 128]
            k2 = qkv[:, D + at : D + at + 128]
            g2 = grad_mixed[:, at : at + 128]
            ps, ds, ds_t = [], [], []
            for side in range(2):
                n = 2 * half + side
                p = probs[group * 4 + n]
                wide = p.astype(f32)
                dp = all_dp[n * TOKENS : n * TOKENS + TOKENS]
                inner = jnp.sum(wide * dp, axis=0, keepdims=True)
                d = (wide * (dp - inner)).astype(bf16)
                ps.append(p)
                ds.append(d)
                ds_t.append(d.T)
            for block, (lhs, rhs) in enumerate(((ds_t, k2), (ds, q2), (ps, g2))):
                both = dot(jnp.concatenate(lhs, axis=0), rhs)
                grad_qkv[:, block * D + at : block * D + at + 128] = jnp.where(
                    low, both[:TOKENS], both[TOKENS:]
                ).astype(bf16)


def attend_back_stacked(qkv, probs, grad_mixed, grad_qkv):
    masks = four_masks(DEPTH ** (-0.5))
    ones = four_masks(1.0)
    low = iota((TOKENS, 2 * DEPTH), 1) < DEPTH
    for group in range(HEADS // 4):
        first = group * 4 * DEPTH
        v4 = qkv[:, 2 * D + first : 2 * D + first + 256]
        g4 = grad_mixed[:, first : first + 256]
        all_dp = dot_t(jnp.concatenate([v4 * mask for mask in masks], axis=0), g4)
        k4 = qkv[:, D + first : D + first + 256]
        slopes = []
        for half in range(2):
            at = first + 128 * half
            q2 = qkv[:, at : at + 128]
            g2 = grad_mixed[:, at : at + 128]
            ps, ds = [], []
            for side in range(2):
                n = 2 * half + side
                p = probs[group * 4 + n]
                wide = p.astype(f32)
                dp = all_dp[n * TOKENS : n * TOKENS + TOKENS]
                inner = jnp.sum(wide * dp, axis=0, keepdims=True)
                d = (wide * (dp - inner)).astype(bf16)
                ps.append(p)
                ds.append(d)
            for block, (lhs, rhs) in enumerate(((ds, q2), (ps, g2))):
                both = dot(jnp.concatenate(lhs, axis=0), rhs)
                grad_qkv[:, (block + 1) * D + at : (block + 1) * D + at + 128] = jnp.where(
                    low, both[:TOKENS], both[TOKENS:]
                ).astype(bf16)
            slopes += ds
        keys = jnp.concatenate([k4 * mask for mask in ones], axis=0)
        grad_qkv[:, first : first + 256] = dot(
            jnp.concatenate(slopes, axis=0).T, keys
        ).astype(bf16)


def norm_back(dh, gain, normed, inverse):
    dn = dh * gain
    first = jnp.mean(dn, axis=-1, keepdims=True)
    second = jnp.mean(dn * normed, axis=-1, keepdims=True)
    return (dn - first - normed * second) * inverse


def pieces(array):
    return [array[index * QUAD : (index + 1) * QUAD] for index in range(4)]


QUARTERS_ONE = ((1, 3), (3, 1), (2, 0), (0, 2))
QUARTERS_TWO = ((2, 0), (0, 2), (3, 1), (1, 3))
FORTH = (1, 0, 2)
BACK = (2, 0, 1)


def ordered(quarters, order):
    return quarters[:1] + tuple(quarters[1 + number] for number in order)


def deal(quarters, c, refs, above, below):
    tops, bottoms = pieces(above), pieces(below)
    even = c == 0
    for (first, second), out in zip(quarters, refs):
        out[...] = jnp.concatenate(
            [jnp.where(even, part[first], part[second]) for part in (tops, bottoms)], axis=0
        ).astype(bf16)


def gather(quarters, c, refs):
    even = c == 0
    values = [ref[...].astype(f32) for ref in refs]
    chosen = []
    for index in range(4):
        at_even = [first for first, _ in quarters].index(index)
        at_odd = [second for _, second in quarters].index(index)
        chosen.append(jnp.where(even, values[at_even], values[at_odd]))
    return (
        jnp.concatenate([value[:QUAD] for value in chosen], axis=0),
        jnp.concatenate([value[QUAD:] for value in chosen], axis=0),
    )


def one_kernel(
    keep, received, gain, weight_qkv, weight_proj, bias,
    stay, first, second, third, u_out, qkv, probs, mixed,
):
    c = parity()
    k = keep[...].astype(f32)
    r = received[...].astype(f32)
    mine = c == 0
    lead = jnp.where(mine, k, r)
    trail = jnp.where(mine, r, k)
    u = jnp.concatenate([lead[:HALF], trail[:HALF]], axis=0)
    g = jnp.concatenate([lead[HALF:], trail[HALF:]], axis=0)
    u_out[...] = u.astype(bf16)
    normed, _ = norm(u)
    h = (normed * row(gain)).astype(bf16)
    qkv[...] = dot(h, weight_qkv[...]).astype(bf16)
    attend(qkv, bias, probs, mixed)
    middle = u + dot(mixed[...], weight_proj[...])
    deal(ordered(QUARTERS_ONE, FORTH), c, (stay, first, second, third), middle, g)


def two_kernel(
    stay, first, second, third, gain, weight_qkv, weight_proj, weight_qkv_t, weight_proj_t, bias,
    back_stay, back_first, back_second, back_third,
    qkv, probs, mixed, grad_mixed, grad_qkv,
):
    c = parity()
    u, g = gather(ordered(QUARTERS_TWO, FORTH), c, (stay, first, second, third))
    normed, inverse = norm(u)
    h = (normed * row(gain)).astype(bf16)
    qkv[...] = dot(h, weight_qkv[...]).astype(bf16)
    attend(qkv, bias, probs, mixed)
    turned = u + dot(mixed[...], weight_proj[...])
    grad_mixed[...] = dot(g.astype(bf16), weight_proj_t[...]).astype(bf16)
    attend_back(qkv, probs, grad_mixed, grad_qkv)
    dh = dot(grad_qkv[...], weight_qkv_t[...])
    du = g + norm_back(dh, row(gain), normed, inverse)
    deal(ordered(QUARTERS_TWO, BACK), c, (back_stay, back_first, back_second, back_third), du, turned)


def three_kernel(
    stay, first, second, third, u, qkv, probs, gain, weight_qkv_t, weight_proj_t,
    keep, send, grad_mixed, grad_qkv,
):
    c = parity()
    g, turned = gather(ordered(QUARTERS_ONE, BACK), c, (stay, first, second, third))
    normed, inverse = norm(u[...].astype(f32))
    grad_mixed[...] = dot(g.astype(bf16), weight_proj_t[...]).astype(bf16)
    attend_back_stacked(qkv, probs, grad_mixed, grad_qkv)
    dh = dot(grad_qkv[...], weight_qkv_t[...])
    du = g + norm_back(dh, row(gain), normed, inverse)
    mine = c == 0
    low = jnp.concatenate([du[:HALF], turned[:HALF]], axis=0)
    high = jnp.concatenate([du[HALF:], turned[HALF:]], axis=0)
    keep[...] = jnp.where(mine, low, high).astype(bf16)
    send[...] = jnp.where(mine, high, low).astype(bf16)


def turn_kernel(weight_qkv, weight_proj, qkv_t, proj_t):
    qkv_t[...] = weight_qkv[...].T
    proj_t[...] = weight_proj[...].T


def shape(*dims, dtype=bf16):
    return jax.ShapeDtypeStruct(dims, dtype)


def call(kernel, outs, scratch, mib, micros, *args, **options):
    return pl.pallas_call(
        kernel,
        out_shape=outs,
        scratch_shapes=scratch,
        compiler_params=pltpu.CompilerParams(vmem_limit_bytes=mib * 1024 * 1024),
        cost_estimate=pl.CostEstimate(
            flops=int(micros * 1e9), bytes_accessed=int(micros * 3e6), transcendentals=0
        ),
        **options,
    )(*args)


def exchange(number, back):
    lats, lons = lax.axis_size("lat"), lax.axis_size("lon")

    def device(a, p, c):
        return a % lats * lons + 2 * p % lons + c

    pairs = []
    for a in range(lats):
        for p in range(lons // 2):
            even, odd = (
                (device(a, p + 1, 0), device(a, p - 1, 1)),
                (device(a - 1, p, 1), device(a, p, 0)),
                (device(a - 1, p - 1, 1), device(a, p + 1, 0)),
            )[number]
            pairs += [(device(a, p, 0), even), (device(a, p, 1), odd)]
    return [(target, source) for source, target in pairs] if back else pairs


def exchanged(values, back):
    return [
        lax.ppermute(value, ("lat", "lon"), exchange(number, back))
        for number, value in zip(BACK if back else FORTH, values)
    ]


def body(
    stream, land, orography, land_vector, orography_table,
    gain_one, qkv_one, proj_one, table_one,
    gain_two, qkv_two, proj_two, table_two, cotangent,
):
    swap = [(i, i ^ 1) for i in range(lax.axis_size("lon"))]
    c = lax.axis_index("lon") % 2

    def flat(array):
        return array.transpose(0, 2, 1, 3).reshape(TOKENS, D)

    def field(array):
        return array.reshape(2, 3, 24, D).transpose(0, 2, 1, 3)

    tokens = shape(TOKENS, D)
    quad = shape(2 * QUAD, D)
    wide = pltpu.VMEM((TOKENS, 3 * D), bf16)
    narrow = pltpu.VMEM((TOKENS, D), bf16)
    keep, send = call(
        pack_kernel, (tokens, tokens),
        [
            narrow, pltpu.VMEM((3, 24), jnp.int32), pltpu.VMEM((3, 24), jnp.int32),
            pltpu.VMEM((D,), f32), pltpu.VMEM((OROG, D), f32), narrow,
            pltpu.SemaphoreType.DMA((6,)),
        ],
        56, 3.0,
        flat(stream), land.T, orography.T, land_vector, orography_table, flat(cotangent),
        in_specs=[pl.BlockSpec(memory_space=pltpu.HBM)] * 6,
    )
    received = lax.ppermute(send, "lon", swap)
    square = shape(HEADS, TOKENS, TOKENS)

    def bias_of(table, masked):
        return call(
            functools.partial(bias_kernel, masked), square,
            [pltpu.VMEM((2, HEADS * 24, 128), f32)] * 2, 8, 1.5,
            lax.dynamic_index_in_dim(table, c, 0, False),
        )

    stay, *leave, u_one, saved_qkv, saved_probs = call(
        one_kernel,
        (quad, quad, quad, quad, tokens, shape(TOKENS, 3 * D), square),
        [narrow], 16, 3.0,
        keep, received, gain_one, qkv_one, proj_one, bias_of(table_one, False),
    )
    table_two, qkv_now, stay = lax.optimization_barrier((table_two, qkv_two, stay))
    turned_shapes = (shape(3 * D, D), shape(D, D))
    qkv_two_t, proj_two_t = call(turn_kernel, turned_shapes, [], 14, 1.5, qkv_now, proj_two)
    arrived = exchanged(leave, False)
    stay, *leave = call(
        two_kernel, (quad, quad, quad, quad),
        [wide, pltpu.VMEM((HEADS, TOKENS, TOKENS), bf16), narrow, narrow, wide], 16, 8.0,
        stay, *arrived, gain_two, qkv_two, proj_two, qkv_two_t, proj_two_t,
        bias_of(table_two, True),
    )
    arrived = exchanged(leave, True)
    qkv_now, stay = lax.optimization_barrier((qkv_one, stay))
    qkv_one_t, proj_one_t = call(turn_kernel, turned_shapes, [], 14, 1.5, qkv_now, proj_one)
    keep, send = call(
        three_kernel, (tokens, tokens), [narrow, wide], 16, 6.0,
        stay, *arrived, u_one, saved_qkv, saved_probs, gain_one, qkv_one_t, proj_one_t,
    )
    received = lax.ppermute(send, "lon", swap)
    output, grad = call(unpack_kernel, (tokens, tokens), [], 8, 1.0, keep, received)
    return field(output), field(grad)


def solution(mesh):
    tokens = P(None, "lat", "lon", None)
    table = P("lat", None, None)
    placed = (
        tokens, P("lat", "lon"), P("lat", "lon"), P(), P(),
        P(), P(), P(), table, P(), P(), P(), table, tokens,
    )
    return jax.shard_map(
        body, mesh=mesh, in_specs=placed, out_specs=(tokens, tokens), check_vma=False
    )
```
